32 devices in a mesh: blk: 16 (over z, y, core), rhs: 2 (over x).
Axes of the slice: x: 2, y: 2, z: 4, core: 2. Of those that a mesh axis runs over, the one named last changes fastest.
Arguments:
- directions: bfloat16 [32768, 256], P('blk', 'rhs'), may hold values from -6 to 6
- axial_pos: bfloat16 [32768], P('blk'), may hold values from 0 to 8
- azimuth: bfloat16 [32768], P('blk'), may hold values from -3.140625 to 3.140625
- panel_area: bfloat16 [32768], P('blk'), may hold values from 0.5 to 2
Outputs:
- product: float32 [32768, 256], P('blk', 'rhs')
- gram: float32 [256, 256], P(None, 'rhs')
The draws below stay inside these ranges and needn't reach their ends.
All inputs are finite; a program needn't handle non-finite values.
Results may differ from the reference program's by a relative error of at most 0.0029.
Values may be sent and summed in bfloat16 or wider, within the bound.
A program may use at most 64 MiB of HBM per device.

```python
import math
import jax
import jax.numpy as jnp
from jax import lax

PAN_DEV = 2048
RHS = 256
ROUNDS = 3
PANELS = 32768
N_BLK = 16


def steps_of(stream_key, shape, pieces, least, high):
    def one(axis_at, shards_of):
        heights = jax.random.uniform(jax.random.fold_in(jax.random.fold_in(stream_key, 6), axis_at), (shards_of,), jnp.float32, least / len(pieces), high / len(pieces))
        return jnp.repeat(jnp.exp(heights), shape[axis_at] // shards_of).reshape((-1,) + (1,) * (len(shape) - axis_at - 1))

    level = one(*pieces[0])
    for cut in pieces[1:]:
        level = level * one(*cut)
    return level


def gaussian(rng, extent, deviation, limit, split=(), held_as=jnp.bfloat16):
    loudness = steps_of(rng, extent, split, -0.22, 0.18) if split else 1.0
    values = jax.random.normal(rng, extent, jnp.float32) * deviation * loudness
    return jnp.minimum(jnp.maximum(values, -limit), limit).astype(held_as)


def setup_inputs(seed: int = 0) -> dict:
    splits = jax.random.split(jax.random.key(seed), 5)
    return {
        "directions": gaussian(splits[0], (PANELS, RHS), 1.0, 6.0, ((0, 16), (1, 2))),
        "axial_pos": jnp.clip(8.0 * jax.random.uniform(splits[1], (PANELS,), jnp.float32) ** steps_of(splits[1], (PANELS,), ((0, 16),), -0.2, 0.2), 0.0, 8.0).astype(jnp.bfloat16),
        "azimuth": jnp.clip(jax.random.uniform(splits[2], (PANELS,), jnp.float32, -3.140625, 3.140625), -3.140625, 3.140625).astype(jnp.bfloat16),
        "panel_area": jnp.clip(jnp.exp(math.log(2.0) - 1.3862944 * jax.random.uniform(splits[3], (PANELS,), jnp.float32) ** steps_of(splits[3], (PANELS,), ((0, 16),), -0.2, 0.2)), 0.5, 2.0).astype(jnp.bfloat16),
    }


def kernel_tile(row_geom, col_geom, count):
    row_axial, row_cos, row_sin, row_weight = row_geom
    col_axial, col_cos, col_sin, col_weight = col_geom
    delta_a = row_axial[:, None] - col_axial[None, :]
    delta_c = row_cos[:, None] - col_cos[None, :]
    delta_s = row_sin[:, None] - col_sin[None, :]
    square = delta_a * delta_a + delta_c * delta_c + delta_s * delta_s
    weights = row_weight[:, None] * col_weight[None, :]
    value = weights * lax.rsqrt(square + 0.01) / jnp.sqrt(jnp.float32(count))
    return value.astype(jnp.bfloat16)

def reference(directions, axial_pos, azimuth, panel_area):
    axial_f = axial_pos.astype(jnp.float32).reshape(N_BLK, PAN_DEV)
    angle_f = azimuth.astype(jnp.float32).reshape(N_BLK, PAN_DEV)
    cos_f = jnp.cos(angle_f)
    sin_f = jnp.sin(angle_f)
    weight_f = panel_area.astype(jnp.float32).reshape(N_BLK, PAN_DEV)
    blocked = directions.astype(jnp.float32).reshape(N_BLK, PAN_DEV, RHS)

    def one_block(index):
        row_geom = (axial_f[index], cos_f[index], sin_f[index], weight_f[index])
        total = jnp.zeros((PAN_DEV, RHS), jnp.float32)
        for offset in range(-ROUNDS, ROUNDS + 1):
            other = ((index + offset) % N_BLK).astype(jnp.int32)
            col_geom = (axial_f[other], cos_f[other], sin_f[other], weight_f[other])
            values = kernel_tile(row_geom, col_geom, PAN_DEV).astype(jnp.float32)
            total = total + jnp.dot(values, blocked[other], precision=lax.Precision.HIGHEST)
        return total
    product = lax.map(one_block, jnp.arange(N_BLK, dtype=jnp.int32)).reshape(PANELS, RHS)
    gram = jnp.dot(directions.astype(jnp.float32).T, product, precision=lax.Precision.HIGHEST) / PANELS
    return (product, gram)
```

```python
import functools

import jax
import jax.numpy as jnp
from jax import lax
from jax.experimental import pallas as pl
from jax.experimental.pallas import tpu as pltpu
from jax.sharding import PartitionSpec as P

MESH = pl.DeviceIdType.MESH
ROW_STEP = 512
COL_STEP = 256
MIDDLE = 4.0
SOFTEN = 0.01
PIECES = 16
SLOTS = 7


def split_three(value):
    high = value.astype(jnp.bfloat16).astype(jnp.float32)
    rest = value - high
    mid = rest.astype(jnp.bfloat16).astype(jnp.float32)
    return high, mid, rest - mid


def panel_kernel(
    n, dirs_ref, geom_ref, product_ref, gram_ref,
    dirs, other, pieces, rows, flat,
    send_dirs, recv_dirs, send_geom, recv_geom, send_other, recv_other,
):
    me = lax.axis_index("blk")
    half = lax.axis_index("rhs")
    count = dirs_ref.shape[0]
    width = dirs_ref.shape[1]
    sign = 1 - 2 * lax.rem(me, 2)

    def block(offset):
        return lax.rem(me + offset * sign + n, n)

    pair = block(1)

    barrier = pltpu.get_barrier_semaphore()
    for offset in (1, -1, 2, -2, 3, -3):
        pl.semaphore_signal(barrier, inc=1, device_id=(block(offset), half), device_id_type=MESH)
    pl.semaphore_signal(barrier, inc=1, device_id=(me, 1 - half), device_id_type=MESH)
    pl.semaphore_wait(barrier, 7)

    targets = ((1, pair), (2, block(-1)), (3, block(2)), (6, block(-3)))

    def dirs_copy(source, slot, target):
        return pltpu.make_async_remote_copy(
            src_ref=source, dst_ref=dirs.at[slot], send_sem=send_dirs.at[slot], recv_sem=recv_dirs.at[slot],
            device_id=(target, half), device_id_type=MESH)

    def geom_copy(source, slot, target):
        return pltpu.make_async_remote_copy(
            src_ref=source, dst_ref=pieces.at[slot], send_sem=send_geom.at[slot], recv_sem=recv_geom.at[slot],
            device_id=(target, half), device_id_type=MESH)

    for slot, target in targets:
        dirs_copy(dirs_ref, slot, target).start()
    across = pltpu.make_async_remote_copy(
        src_ref=dirs_ref, dst_ref=other, send_sem=send_other, recv_sem=recv_other,
        device_id=(me, 1 - half), device_id_type=MESH)
    across.start()

    axial = geom_ref[0:1, :] - MIDDLE
    cosine = geom_ref[1:2, :]
    sine = geom_ref[2:3, :]
    weight = geom_ref[3:4, :]
    scale = 1.0 / (weight * weight)
    norm = axial * axial + cosine * cosine + sine * sine + 0.5 * SOFTEN
    col_parts = (scale, norm * scale, axial * scale, cosine * scale, sine * scale)
    row_scale = scale * float(count)
    row_parts = (norm * row_scale, row_scale, -2.0 * axial * row_scale, -2.0 * cosine * row_scale,
                 -2.0 * sine * row_scale)
    flat[...] = jnp.zeros_like(flat)
    for at, part in enumerate(col_parts):
        for level, piece in enumerate(split_three(part)):
            flat[3 * at + level:3 * at + level + 1, :] = piece
    pieces[0] = flat[0:PIECES, :].astype(jnp.bfloat16)
    for slot, target in targets:
        geom_copy(pieces.at[0], slot, target).start()
    dirs[0] = dirs_ref[...]

    flat[...] = jnp.zeros_like(flat)
    for at, part in enumerate(row_parts):
        for level, piece in enumerate(split_three(part)):
            for spot in range(3):
                place = PIECES * level + 3 * at + spot
                flat[place:place + 1, :] = piece
    for start in range(0, count, 128):
        turned = flat[:, start:start + 128].T
        rows[start:start + 128, :] = turned[:, :3 * PIECES].astype(jnp.bfloat16)
    product_ref[...] = jnp.zeros_like(product_ref)

    def tile(slot):
        def step(at, carry):
            here = pl.ds(pl.multiple_of(at * ROW_STEP, ROW_STEP), ROW_STEP)
            row_feature = rows[here, :]
            total = product_ref[here, :]
            for start in range(0, count, COL_STEP):
                part = pieces[slot, :, start:start + COL_STEP]
                col_feature = jnp.concatenate([part, part, part], axis=0)
                square = jnp.dot(row_feature, col_feature, preferred_element_type=jnp.float32)
                values = lax.rsqrt(square).astype(jnp.bfloat16)
                total = total + jnp.dot(
                    values, dirs[slot, start:start + COL_STEP, :], preferred_element_type=jnp.float32)
            product_ref[here, :] = total
            return carry

        lax.fori_loop(0, count // ROW_STEP, step, 0)

    def turn(slot, carry):
        @pl.when(slot > 0)
        def _():
            dirs_copy(dirs_ref, slot, pair).wait_recv()
            geom_copy(pieces.at[0], slot, pair).wait_recv()

        @pl.when((slot == 2) | (slot == 3))
        def _():
            dirs_copy(dirs.at[slot], slot + 2, pair).start()
            geom_copy(pieces.at[slot], slot + 2, pair).start()

        tile(slot)
        return carry

    lax.fori_loop(0, SLOTS, turn, 0)

    across.wait()
    total = product_ref[...]
    high = total.astype(jnp.bfloat16)
    low = (total - high.astype(jnp.float32)).astype(jnp.bfloat16)
    inverse = 1.0 / (count * n)
    for place, value in ((half, dirs[0]), (1 - half, other[...])):
        turned = value.T
        inner = jnp.dot(turned, high, preferred_element_type=jnp.float32)
        inner = inner + jnp.dot(turned, low, preferred_element_type=jnp.float32)
        gram_ref[pl.ds(pl.multiple_of(place * width, width), width), :] = inner * inverse

    for slot in range(1, SLOTS):
        dirs_copy(dirs_ref, slot, pair).wait_send()
        geom_copy(pieces.at[0], slot, pair).wait_send()


def shards(n, directions, axial_pos, azimuth, panel_area):
    count, width = directions.shape
    angle = azimuth.astype(jnp.float32)
    geom = jnp.stack([axial_pos.astype(jnp.float32), jnp.cos(angle), jnp.sin(angle), panel_area.astype(jnp.float32)])
    vmem = pl.BlockSpec(memory_space=pltpu.VMEM)
    product, gram = pl.pallas_call(
        functools.partial(panel_kernel, n),
        out_shape=(
            jax.ShapeDtypeStruct((count, width), jnp.float32),
            jax.ShapeDtypeStruct((2 * width, width), jnp.float32),
        ),
        in_specs=[vmem, vmem],
        out_specs=(vmem, vmem),
        scratch_shapes=[
            pltpu.VMEM((SLOTS, count, width), jnp.bfloat16),
            pltpu.VMEM((count, width), jnp.bfloat16),
            pltpu.VMEM((SLOTS, PIECES, count), jnp.bfloat16),
            pltpu.VMEM((count, 3 * PIECES), jnp.bfloat16),
            pltpu.VMEM((128, count), jnp.float32),
            pltpu.SemaphoreType.DMA((SLOTS,)),
            pltpu.SemaphoreType.DMA((SLOTS,)),
            pltpu.SemaphoreType.DMA((SLOTS,)),
            pltpu.SemaphoreType.DMA((SLOTS,)),
            pltpu.SemaphoreType.DMA,
            pltpu.SemaphoreType.DMA,
        ],
        compiler_params=pltpu.CompilerParams(
            collective_id=0, has_side_effects=True, vmem_limit_bytes=48 * 1024 * 1024),
        cost_estimate=pl.CostEstimate(
            flops=SLOTS * 2 * count * count * (width + 48), bytes_accessed=4 * count * width,
            transcendentals=SLOTS * count * count),
        name="panels",
    )(directions, geom)
    return product, lax.psum(gram, "blk")


def solution(mesh):
    in_specs = (P("blk", "rhs"), P("blk"), P("blk"), P("blk"))
    out_specs = (P("blk", "rhs"), P(None, "rhs"))
    body = functools.partial(shards, mesh.shape["blk"])
    return jax.shard_map(body, mesh=mesh, in_specs=in_specs, out_specs=out_specs, check_vma=False)
```

```python
import functools

import jax
import jax.numpy as jnp
from jax import lax
from jax.experimental import pallas as pl
from jax.experimental.pallas import tpu as pltpu
from jax.sharding import PartitionSpec as P

MESH = pl.DeviceIdType.MESH
ROW_STEP = 512
COL_STEP = 512
MIDDLE = 4.0
SOFTEN = 0.01
PIECES = 16
SLOTS = 7


def split_three(value):
    high = value.astype(jnp.bfloat16).astype(jnp.float32)
    rest = value - high
    mid = rest.astype(jnp.bfloat16).astype(jnp.float32)
    return high, mid, rest - mid


def panel_kernel(
    n, reduce_here, dirs_ref, geom_ref, product_ref, gram_ref,
    dirs, other, pieces, rows, flat, partial, landed, summed,
    send_dirs, recv_dirs, send_geom, recv_geom, send_other, recv_other,
    send_part, recv_part, send_sum, recv_sum,
):
    me = lax.axis_index("blk")
    half = lax.axis_index("rhs")
    count = dirs_ref.shape[0]
    width = dirs_ref.shape[1]
    sign = 1 - 2 * lax.rem(me, 2)

    def block(offset):
        return lax.rem(me + offset * sign + n, n)

    pair = block(1)

    barrier = pltpu.get_barrier_semaphore()
    pl.semaphore_signal(barrier, inc=1, device_id=(me, 1 - half), device_id_type=MESH)
    if reduce_here:
        def greet(step, carry):
            pl.semaphore_signal(barrier, inc=1, device_id=(lax.rem(me + step, n), half), device_id_type=MESH)
            return carry

        lax.fori_loop(1, n, greet, 0)
        pl.semaphore_wait(barrier, n)
    else:
        for offset in (1, -1, 2, -2, 3, -3):
            pl.semaphore_signal(barrier, inc=1, device_id=(block(offset), half), device_id_type=MESH)
        pl.semaphore_wait(barrier, 7)

    targets = ((1, pair), (2, block(-1)), (3, block(2)), (6, block(-3)))

    def dirs_copy(source, slot, target):
        return pltpu.make_async_remote_copy(
            src_ref=source, dst_ref=dirs.at[slot], send_sem=send_dirs.at[slot], recv_sem=recv_dirs.at[slot],
            device_id=(target, half), device_id_type=MESH)

    def geom_copy(source, slot, target):
        return pltpu.make_async_remote_copy(
            src_ref=source, dst_ref=pieces.at[slot], send_sem=send_geom.at[slot], recv_sem=recv_geom.at[slot],
            device_id=(target, half), device_id_type=MESH)

    for slot, target in targets:
        dirs_copy(dirs_ref, slot, target).start()
    across = pltpu.make_async_remote_copy(
        src_ref=dirs_ref, dst_ref=other, send_sem=send_other, recv_sem=recv_other,
        device_id=(me, 1 - half), device_id_type=MESH)
    across.start()

    axial = geom_ref[0:1, :] - MIDDLE
    cosine = geom_ref[1:2, :]
    sine = geom_ref[2:3, :]
    weight = geom_ref[3:4, :]
    scale = 1.0 / (weight * weight)
    norm = axial * axial + cosine * cosine + sine * sine + 0.5 * SOFTEN
    col_parts = (scale, norm * scale, axial * scale, cosine * scale, sine * scale)
    row_scale = scale * float(count)
    row_parts = (norm * row_scale, row_scale, -2.0 * axial * row_scale, -2.0 * cosine * row_scale,
                 -2.0 * sine * row_scale)
    flat[...] = jnp.zeros_like(flat)
    for at, part in enumerate(col_parts):
        for level, piece in enumerate(split_three(part)):
            flat[3 * at + level:3 * at + level + 1, :] = piece
    pieces[0] = flat[0:PIECES, :].astype(jnp.bfloat16)
    for slot, target in targets:
        geom_copy(pieces.at[0], slot, target).start()
    dirs[0] = dirs_ref[...]

    flat[...] = jnp.zeros_like(flat)
    for at, part in enumerate(row_parts):
        for level, piece in enumerate(split_three(part)):
            for spot in range(3):
                place = PIECES * level + 3 * at + spot
                flat[place:place + 1, :] = piece
    for start in range(0, count, 128):
        turned = flat[:, start:start + 128].T
        rows[start:start + 128, :] = turned[:, :3 * PIECES].astype(jnp.bfloat16)
    product_ref[...] = jnp.zeros_like(product_ref)

    def tile(slot):
        def step(at, carry):
            here = pl.ds(pl.multiple_of(at * ROW_STEP, ROW_STEP), ROW_STEP)
            row_feature = rows[here, :]
            total = product_ref[here, :]
            def squares(start):
                part = pieces[slot, :, start:start + COL_STEP]
                col_feature = jnp.concatenate([part, part, part], axis=0)
                return jnp.dot(row_feature, col_feature, preferred_element_type=jnp.float32)

            square = squares(0)
            for start in range(0, count, COL_STEP):
                ahead = squares(start + COL_STEP) if start + COL_STEP < count else None
                values = lax.rsqrt(square).astype(jnp.bfloat16)
                total = total + jnp.dot(
                    values, dirs[slot, start:start + COL_STEP, :], preferred_element_type=jnp.float32)
                square = ahead
            product_ref[here, :] = total
            return carry

        lax.fori_loop(0, count // ROW_STEP, step, 0)

    def turn(slot, carry):
        @pl.when(slot > 0)
        def _():
            dirs_copy(dirs_ref, slot, pair).wait_recv()
            geom_copy(pieces.at[0], slot, pair).wait_recv()

        @pl.when((slot == 2) | (slot == 3))
        def _():
            dirs_copy(dirs.at[slot], slot + 2, pair).start()
            geom_copy(pieces.at[slot], slot + 2, pair).start()

        tile(slot)
        return carry

    lax.fori_loop(0, SLOTS, turn, 0)

    across.wait()
    total = product_ref[...]
    high = total.astype(jnp.bfloat16)
    low = (total - high.astype(jnp.float32)).astype(jnp.bfloat16)
    inverse = 1.0 / (count * n)
    for place, value in ((half, dirs[0]), (1 - half, other[...])):
        turned = value.T
        inner = jnp.dot(turned, high, preferred_element_type=jnp.float32)
        inner = inner + jnp.dot(turned, low, preferred_element_type=jnp.float32)
        partial[pl.ds(pl.multiple_of(place * width, width), width), :] = inner * inverse

    if reduce_here:
        depth = landed.shape[1]

        def rows_of(owner):
            return pl.ds(pl.multiple_of(owner * depth, depth), depth)

        def part_copy(step):
            target = lax.rem(me + step, n)
            return pltpu.make_async_remote_copy(
                src_ref=partial.at[rows_of(target)], dst_ref=landed.at[step],
                send_sem=send_part.at[step], recv_sem=recv_part.at[step],
                device_id=(target, half), device_id_type=MESH)

        def sum_copy(step):
            target = lax.rem(me + step, n)
            return pltpu.make_async_remote_copy(
                src_ref=summed.at[rows_of(me)], dst_ref=summed.at[rows_of(me)],
                send_sem=send_sum.at[step], recv_sem=recv_sum.at[step],
                device_id=(target, half), device_id_type=MESH)

        def each(act):
            def run(step, carry):
                act(step)
                return carry

            lax.fori_loop(1, n, run, 0)

        each(lambda step: part_copy(step).start())
        landed[0] = partial[rows_of(me), :]
        each(lambda step: part_copy(step).wait_recv())
        summed[rows_of(me), :] = jnp.sum(landed[...], axis=0)
        each(lambda step: sum_copy(step).start())
        each(lambda step: sum_copy(step).wait_recv())
        gram_ref[...] = summed[...]
        each(lambda step: part_copy(step).wait_send())
        each(lambda step: sum_copy(step).wait_send())
    else:
        gram_ref[...] = partial[...]

    for slot in range(1, SLOTS):
        dirs_copy(dirs_ref, slot, pair).wait_send()
        geom_copy(pieces.at[0], slot, pair).wait_send()


def shards(n, directions, axial_pos, azimuth, panel_area):
    count, width = directions.shape
    angle = azimuth.astype(jnp.float32)
    geom = jnp.stack([axial_pos.astype(jnp.float32), jnp.cos(angle), jnp.sin(angle), panel_area.astype(jnp.float32)])
    vmem = pl.BlockSpec(memory_space=pltpu.VMEM)
    reduce_here = (2 * width) % (8 * n) == 0
    depth = 2 * width // n if reduce_here else 8
    product, gram = pl.pallas_call(
        functools.partial(panel_kernel, n, reduce_here),
        out_shape=(
            jax.ShapeDtypeStruct((count, width), jnp.float32),
            jax.ShapeDtypeStruct((2 * width, width), jnp.float32),
        ),
        in_specs=[vmem, vmem],
        out_specs=(vmem, vmem),
        scratch_shapes=[
            pltpu.VMEM((SLOTS, count, width), jnp.bfloat16),
            pltpu.VMEM((count, width), jnp.bfloat16),
            pltpu.VMEM((SLOTS, PIECES, count), jnp.bfloat16),
            pltpu.VMEM((count, 3 * PIECES), jnp.bfloat16),
            pltpu.VMEM((128, count), jnp.float32),
            pltpu.VMEM((2 * width, width), jnp.float32),
            pltpu.VMEM((n, depth, width), jnp.float32),
            pltpu.VMEM((2 * width, width), jnp.float32),
            pltpu.SemaphoreType.DMA((SLOTS,)),
            pltpu.SemaphoreType.DMA((SLOTS,)),
            pltpu.SemaphoreType.DMA((SLOTS,)),
            pltpu.SemaphoreType.DMA((SLOTS,)),
            pltpu.SemaphoreType.DMA,
            pltpu.SemaphoreType.DMA,
            pltpu.SemaphoreType.DMA((n,)),
            pltpu.SemaphoreType.DMA((n,)),
            pltpu.SemaphoreType.DMA((n,)),
            pltpu.SemaphoreType.DMA((n,)),
        ],
        compiler_params=pltpu.CompilerParams(
            collective_id=0, has_side_effects=True, vmem_limit_bytes=48 * 1024 * 1024),
        cost_estimate=pl.CostEstimate(
            flops=SLOTS * 2 * count * count * (width + 48), bytes_accessed=4 * count * width,
            transcendentals=SLOTS * count * count),
        name="panels",
    )(directions, geom)
    return product, gram if reduce_here else lax.psum(gram, "blk")


def solution(mesh):
    in_specs = (P("blk", "rhs"), P("blk"), P("blk"), P("blk"))
    out_specs = (P("blk", "rhs"), P(None, "rhs"))
    body = functools.partial(shards, mesh.shape["blk"])
    return jax.shard_map(body, mesh=mesh, in_specs=in_specs, out_specs=out_specs, check_vma=False)
```

```python
import functools

import jax
import jax.numpy as jnp
from jax import lax
from jax.experimental import pallas as pl
from jax.experimental.pallas import tpu as pltpu
from jax.sharding import PartitionSpec as P

MESH = pl.DeviceIdType.MESH
ROW_STEP = 512
COL_STEP = 512
MIDDLE = 4.0
SOFTEN = 0.01
PIECES = 16
SLOTS = 7


def split_three(value):
    high = value.astype(jnp.bfloat16).astype(jnp.float32)
    rest = value - high
    mid = rest.astype(jnp.bfloat16).astype(jnp.float32)
    return high, mid, rest - mid


def inverse_root(four_square):
    first = lax.rsqrt(four_square.astype(jnp.bfloat16)).astype(jnp.float32)
    return (first * (3.0 - four_square * first * first)).astype(jnp.bfloat16)


def panel_kernel(
    n, reduce_here, dirs_ref, geom_ref, product_ref, gram_ref,
    dirs, other, pieces, rows, flat, partial, landed, summed,
    send_dirs, recv_dirs, send_geom, recv_geom, send_other, recv_other,
    send_part, recv_part, send_sum, recv_sum,
):
    me = lax.axis_index("blk")
    half = lax.axis_index("rhs")
    count = dirs_ref.shape[0]
    width = dirs_ref.shape[1]
    sign = 1 - 2 * lax.rem(me, 2)

    def block(offset):
        return lax.rem(me + offset * sign + n, n)

    pair = block(1)

    barrier = pltpu.get_barrier_semaphore()
    pl.semaphore_signal(barrier, inc=1, device_id=(me, 1 - half), device_id_type=MESH)
    if reduce_here:
        def greet(step, carry):
            pl.semaphore_signal(barrier, inc=1, device_id=(lax.rem(me + step, n), half), device_id_type=MESH)
            return carry

        lax.fori_loop(1, n, greet, 0)
        pl.semaphore_wait(barrier, n)
    else:
        for offset in (1, -1, 2, -2, 3, -3):
            pl.semaphore_signal(barrier, inc=1, device_id=(block(offset), half), device_id_type=MESH)
        pl.semaphore_wait(barrier, 7)

    targets = ((1, pair), (2, block(-1)), (3, block(2)), (6, block(-3)))

    def dirs_copy(source, slot, target):
        return pltpu.make_async_remote_copy(
            src_ref=source, dst_ref=dirs.at[slot], send_sem=send_dirs.at[slot], recv_sem=recv_dirs.at[slot],
            device_id=(target, half), device_id_type=MESH)

    def geom_copy(source, slot, target):
        return pltpu.make_async_remote_copy(
            src_ref=source, dst_ref=pieces.at[slot], send_sem=send_geom.at[slot], recv_sem=recv_geom.at[slot],
            device_id=(target, half), device_id_type=MESH)

    for slot, target in targets:
        dirs_copy(dirs_ref, slot, target).start()
    across = pltpu.make_async_remote_copy(
        src_ref=dirs_ref, dst_ref=other, send_sem=send_other, recv_sem=recv_other,
        device_id=(me, 1 - half), device_id_type=MESH)
    across.start()

    axial = geom_ref[0:1, :] - MIDDLE
    cosine = geom_ref[1:2, :]
    sine = geom_ref[2:3, :]
    weight = geom_ref[3:4, :]
    scale = 1.0 / (weight * weight)
    norm = axial * axial + cosine * cosine + sine * sine + 0.5 * SOFTEN
    col_parts = (scale, norm * scale, axial * scale, cosine * scale, sine * scale)
    row_scale = scale * (4.0 * count)
    row_parts = (norm * row_scale, row_scale, -2.0 * axial * row_scale, -2.0 * cosine * row_scale,
                 -2.0 * sine * row_scale)
    flat[...] = jnp.zeros_like(flat)
    for at, part in enumerate(col_parts):
        for level, piece in enumerate(split_three(part)):
            flat[3 * at + level:3 * at + level + 1, :] = piece
    pieces[0] = flat[0:PIECES, :].astype(jnp.bfloat16)
    for slot, target in targets:
        geom_copy(pieces.at[0], slot, target).start()
    dirs[0] = dirs_ref[...]

    flat[...] = jnp.zeros_like(flat)
    for at, part in enumerate(row_parts):
        for level, piece in enumerate(split_three(part)):
            for spot in range(3):
                place = PIECES * level + 3 * at + spot
                flat[place:place + 1, :] = piece
    for start in range(0, count, 128):
        turned = flat[:, start:start + 128].T
        rows[start:start + 128, :] = turned[:, :3 * PIECES].astype(jnp.bfloat16)
    product_ref[...] = jnp.zeros_like(product_ref)

    def tile(slot):
        def step(at, carry):
            here = pl.ds(pl.multiple_of(at * ROW_STEP, ROW_STEP), ROW_STEP)
            row_feature = rows[here, :]
            total = product_ref[here, :]
            def squares(start):
                part = pieces[slot, :, start:start + COL_STEP]
                col_feature = jnp.concatenate([part, part, part], axis=0)
                return jnp.dot(row_feature, col_feature, preferred_element_type=jnp.float32)

            square = squares(0)
            for start in range(0, count, COL_STEP):
                ahead = squares(start + COL_STEP) if start + COL_STEP < count else None
                values = inverse_root(square)
                total = total + jnp.dot(
                    values, dirs[slot, start:start + COL_STEP, :], preferred_element_type=jnp.float32)
                square = ahead
            product_ref[here, :] = total
            return carry

        lax.fori_loop(0, count // ROW_STEP, step, 0)

    def turn(slot, carry):
        @pl.when(slot > 0)
        def _():
            dirs_copy(dirs_ref, slot, pair).wait_recv()
            geom_copy(pieces.at[0], slot, pair).wait_recv()

        @pl.when((slot == 2) | (slot == 3))
        def _():
            dirs_copy(dirs.at[slot], slot + 2, pair).start()
            geom_copy(pieces.at[slot], slot + 2, pair).start()

        tile(slot)
        return carry

    lax.fori_loop(0, SLOTS, turn, 0)

    across.wait()
    total = product_ref[...]
    high = total.astype(jnp.bfloat16)
    low = (total - high.astype(jnp.float32)).astype(jnp.bfloat16)
    inverse = 1.0 / (count * n)
    for place, value in ((half, dirs[0]), (1 - half, other[...])):
        turned = value.T
        inner = jnp.dot(turned, high, preferred_element_type=jnp.float32)
        inner = inner + jnp.dot(turned, low, preferred_element_type=jnp.float32)
        partial[pl.ds(pl.multiple_of(place * width, width), width), :] = inner * inverse

    if reduce_here:
        depth = landed.shape[1]

        def rows_of(owner):
            return pl.ds(pl.multiple_of(owner * depth, depth), depth)

        def part_copy(step):
            target = lax.rem(me + step, n)
            return pltpu.make_async_remote_copy(
                src_ref=partial.at[rows_of(target)], dst_ref=landed.at[step],
                send_sem=send_part.at[step], recv_sem=recv_part.at[step],
                device_id=(target, half), device_id_type=MESH)

        def sum_copy(step):
            target = lax.rem(me + step, n)
            return pltpu.make_async_remote_copy(
                src_ref=summed.at[rows_of(me)], dst_ref=summed.at[rows_of(me)],
                send_sem=send_sum.at[step], recv_sem=recv_sum.at[step],
                device_id=(target, half), device_id_type=MESH)

        def each(act):
            def run(step, carry):
                act(step)
                return carry

            lax.fori_loop(1, n, run, 0)

        each(lambda step: part_copy(step).start())
        landed[0] = partial[rows_of(me), :]
        each(lambda step: part_copy(step).wait_recv())
        summed[rows_of(me), :] = jnp.sum(landed[...], axis=0)
        each(lambda step: sum_copy(step).start())
        each(lambda step: sum_copy(step).wait_recv())
        gram_ref[...] = summed[...]
        each(lambda step: part_copy(step).wait_send())
        each(lambda step: sum_copy(step).wait_send())
    else:
        gram_ref[...] = partial[...]

    for slot in range(1, SLOTS):
        dirs_copy(dirs_ref, slot, pair).wait_send()
        geom_copy(pieces.at[0], slot, pair).wait_send()


def shards(n, directions, axial_pos, azimuth, panel_area):
    count, width = directions.shape
    angle = azimuth.astype(jnp.float32)
    geom = jnp.stack([axial_pos.astype(jnp.float32), jnp.cos(angle), jnp.sin(angle), panel_area.astype(jnp.float32)])
    vmem = pl.BlockSpec(memory_space=pltpu.VMEM)
    reduce_here = (2 * width) % (8 * n) == 0
    depth = 2 * width // n if reduce_here else 8
    product, gram = pl.pallas_call(
        functools.partial(panel_kernel, n, reduce_here),
        out_shape=(
            jax.ShapeDtypeStruct((count, width), jnp.float32),
            jax.ShapeDtypeStruct((2 * width, width), jnp.float32),
        ),
        in_specs=[vmem, vmem],
        out_specs=(vmem, vmem),
        scratch_shapes=[
            pltpu.VMEM((SLOTS, count, width), jnp.bfloat16),
            pltpu.VMEM((count, width), jnp.bfloat16),
            pltpu.VMEM((SLOTS, PIECES, count), jnp.bfloat16),
            pltpu.VMEM((count, 3 * PIECES), jnp.bfloat16),
            pltpu.VMEM((128, count), jnp.float32),
            pltpu.VMEM((2 * width, width), jnp.float32),
            pltpu.VMEM((n, depth, width), jnp.float32),
            pltpu.VMEM((2 * width, width), jnp.float32),
            pltpu.SemaphoreType.DMA((SLOTS,)),
            pltpu.SemaphoreType.DMA((SLOTS,)),
            pltpu.SemaphoreType.DMA((SLOTS,)),
            pltpu.SemaphoreType.DMA((SLOTS,)),
            pltpu.SemaphoreType.DMA,
            pltpu.SemaphoreType.DMA,
            pltpu.SemaphoreType.DMA((n,)),
            pltpu.SemaphoreType.DMA((n,)),
            pltpu.SemaphoreType.DMA((n,)),
            pltpu.SemaphoreType.DMA((n,)),
        ],
        compiler_params=pltpu.CompilerParams(
            collective_id=0, has_side_effects=True, vmem_limit_bytes=48 * 1024 * 1024),
        cost_estimate=pl.CostEstimate(
            flops=SLOTS * 2 * count * count * (width + 48), bytes_accessed=4 * count * width,
            transcendentals=SLOTS * count * count),
        name="panels",
    )(directions, geom)
    return product, gram if reduce_here else lax.psum(gram, "blk")


def solution(mesh):
    in_specs = (P("blk", "rhs"), P("blk"), P("blk"), P("blk"))
    out_specs = (P("blk", "rhs"), P(None, "rhs"))
    body = functools.partial(shards, mesh.shape["blk"])
    return jax.shard_map(body, mesh=mesh, in_specs=in_specs, out_specs=out_specs, check_vma=False)
```

```python
import functools

import jax
import jax.numpy as jnp
from jax import lax
from jax.experimental import pallas as pl
from jax.experimental.pallas import tpu as pltpu
from jax.sharding import PartitionSpec as P

MESH = pl.DeviceIdType.MESH
ROW_STEP = 256
SUB_STEP = 16
COL_STEP = 512
MIDDLE = 4.0
SOFTEN = 0.01
FEATURES = 8
SLOTS = 7


def panel_kernel(
    n, reduce_here, dirs_ref, geom_ref, product_ref, gram_ref,
    dirs, other, pieces, rows, columns, flat, partial, landed, summed,
    send_dirs, recv_dirs, send_geom, recv_geom, send_other, recv_other,
    send_part, recv_part, send_sum, recv_sum,
):
    me = lax.axis_index("blk")
    half = lax.axis_index("rhs")
    count = dirs_ref.shape[0]
    width = dirs_ref.shape[1]
    sign = 1 - 2 * lax.rem(me, 2)

    def block(offset):
        return lax.rem(me + offset * sign + n, n)

    pair = block(1)

    barrier = pltpu.get_barrier_semaphore()
    pl.semaphore_signal(barrier, inc=1, device_id=(me, 1 - half), device_id_type=MESH)
    if reduce_here:
        def greet(step, carry):
            pl.semaphore_signal(barrier, inc=1, device_id=(lax.rem(me + step, n), half), device_id_type=MESH)
            return carry

        lax.fori_loop(1, n, greet, 0)
        pl.semaphore_wait(barrier, n)
    else:
        for offset in (1, -1, 2, -2, 3, -3):
            pl.semaphore_signal(barrier, inc=1, device_id=(block(offset), half), device_id_type=MESH)
        pl.semaphore_wait(barrier, 7)

    targets = ((1, pair), (2, block(-1)), (3, block(2)), (6, block(-3)))

    def dirs_copy(source, slot, target):
        return pltpu.make_async_remote_copy(
            src_ref=source, dst_ref=dirs.at[slot], send_sem=send_dirs.at[slot], recv_sem=recv_dirs.at[slot],
            device_id=(target, half), device_id_type=MESH)

    def geom_copy(source, slot, target):
        return pltpu.make_async_remote_copy(
            src_ref=source, dst_ref=pieces.at[slot], send_sem=send_geom.at[slot], recv_sem=recv_geom.at[slot],
            device_id=(target, half), device_id_type=MESH)

    for slot, target in targets:
        dirs_copy(dirs_ref, slot, target).start()
    across = pltpu.make_async_remote_copy(
        src_ref=dirs_ref, dst_ref=other, send_sem=send_other, recv_sem=recv_other,
        device_id=(me, 1 - half), device_id_type=MESH)
    across.start()

    axial = geom_ref[0:1, :] - MIDDLE
    cosine = geom_ref[1:2, :]
    sine = geom_ref[2:3, :]
    weight = geom_ref[3:4, :]
    scale = 1.0 / (weight * weight)
    norm = axial * axial + cosine * cosine + sine * sine + 0.5 * SOFTEN
    col_parts = (scale, norm * scale, axial * scale, cosine * scale, sine * scale)
    row_scale = scale * float(count)
    row_parts = (norm * row_scale, row_scale, -2.0 * axial * row_scale, -2.0 * cosine * row_scale,
                 -2.0 * sine * row_scale)
    flat[...] = jnp.zeros_like(flat)
    for at, part in enumerate(col_parts):
        flat[at:at + 1, :] = part
    pieces[0] = flat[0:FEATURES, :]
    for slot, target in targets:
        geom_copy(pieces.at[0], slot, target).start()
    dirs[0] = dirs_ref[...]

    for at, part in enumerate(row_parts):
        flat[at:at + 1, :] = part
    for start in range(0, count, 128):
        turned = flat[:, start:start + 128].T
        for at in range(len(row_parts)):
            rows[at, start:start + 128, :] = jnp.broadcast_to(turned[:, at:at + 1], (128, 128))
    product_ref[...] = jnp.zeros_like(product_ref)

    def tile(slot):
        for at in range(len(col_parts)):
            columns[at] = jnp.broadcast_to(pieces[slot, at:at + 1, :], (SUB_STEP, count))

        def step(at, carry):
            base = pl.multiple_of(at * ROW_STEP, ROW_STEP)
            here = pl.ds(base, ROW_STEP)
            total = product_ref[here, :]
            for start in range(0, count, COL_STEP):
                strips = []
                for sub in range(0, ROW_STEP, SUB_STEP):
                    square = None
                    for part in range(len(col_parts)):
                        row = rows[part, pl.ds(pl.multiple_of(base + sub, SUB_STEP), SUB_STEP), :]
                        row = jnp.concatenate([row] * (COL_STEP // 128), axis=1)
                        term = row * columns[part, :, start:start + COL_STEP]
                        square = term if square is None else square + term
                    strips.append(lax.rsqrt(square).astype(jnp.bfloat16))
                values = jnp.concatenate(strips, axis=0)
                total = total + jnp.dot(
                    values, dirs[slot, start:start + COL_STEP, :], preferred_element_type=jnp.float32)
            product_ref[here, :] = total
            return carry

        lax.fori_loop(0, count // ROW_STEP, step, 0)

    def turn(slot, carry):
        @pl.when(slot > 0)
        def _():
            dirs_copy(dirs_ref, slot, pair).wait_recv()
            geom_copy(pieces.at[0], slot, pair).wait_recv()

        @pl.when((slot == 2) | (slot == 3))
        def _():
            dirs_copy(dirs.at[slot], slot + 2, pair).start()
            geom_copy(pieces.at[slot], slot + 2, pair).start()

        tile(slot)
        return carry

    lax.fori_loop(0, SLOTS, turn, 0)

    across.wait()
    total = product_ref[...]
    high = total.astype(jnp.bfloat16)
    low = (total - high.astype(jnp.float32)).astype(jnp.bfloat16)
    inverse = 1.0 / (count * n)
    for place, value in ((half, dirs[0]), (1 - half, other[...])):
        turned = value.T
        inner = jnp.dot(turned, high, preferred_element_type=jnp.float32)
        inner = inner + jnp.dot(turned, low, preferred_element_type=jnp.float32)
        partial[pl.ds(pl.multiple_of(place * width, width), width), :] = inner * inverse

    if reduce_here:
        depth = landed.shape[1]

        def rows_of(owner):
            return pl.ds(pl.multiple_of(owner * depth, depth), depth)

        def part_copy(step):
            target = lax.rem(me + step, n)
            return pltpu.make_async_remote_copy(
                src_ref=partial.at[rows_of(target)], dst_ref=landed.at[step],
                send_sem=send_part.at[step], recv_sem=recv_part.at[step],
                device_id=(target, half), device_id_type=MESH)

        def sum_copy(step):
            target = lax.rem(me + step, n)
            return pltpu.make_async_remote_copy(
                src_ref=summed.at[rows_of(me)], dst_ref=summed.at[rows_of(me)],
                send_sem=send_sum.at[step], recv_sem=recv_sum.at[step],
                device_id=(target, half), device_id_type=MESH)

        def each(act):
            def run(step, carry):
                act(step)
                return carry

            lax.fori_loop(1, n, run, 0)

        each(lambda step: part_copy(step).start())
        landed[0] = partial[rows_of(me), :]
        each(lambda step: part_copy(step).wait_recv())
        summed[rows_of(me), :] = jnp.sum(landed[...], axis=0)
        each(lambda step: sum_copy(step).start())
        each(lambda step: sum_copy(step).wait_recv())
        gram_ref[...] = summed[...]
        each(lambda step: part_copy(step).wait_send())
        each(lambda step: sum_copy(step).wait_send())
    else:
        gram_ref[...] = partial[...]

    for slot in range(1, SLOTS):
        dirs_copy(dirs_ref, slot, pair).wait_send()
        geom_copy(pieces.at[0], slot, pair).wait_send()


def shards(n, directions, axial_pos, azimuth, panel_area):
    count, width = directions.shape
    angle = azimuth.astype(jnp.float32)
    geom = jnp.stack([axial_pos.astype(jnp.float32), jnp.cos(angle), jnp.sin(angle), panel_area.astype(jnp.float32)])
    vmem = pl.BlockSpec(memory_space=pltpu.VMEM)
    reduce_here = (2 * width) % (8 * n) == 0
    depth = 2 * width // n if reduce_here else 8
    product, gram = pl.pallas_call(
        functools.partial(panel_kernel, n, reduce_here),
        out_shape=(
            jax.ShapeDtypeStruct((count, width), jnp.float32),
            jax.ShapeDtypeStruct((2 * width, width), jnp.float32),
        ),
        in_specs=[vmem, vmem],
        out_specs=(vmem, vmem),
        scratch_shapes=[
            pltpu.VMEM((SLOTS, count, width), jnp.bfloat16),
            pltpu.VMEM((count, width), jnp.bfloat16),
            pltpu.VMEM((SLOTS, FEATURES, count), jnp.float32),
            pltpu.VMEM((5, count, 128), jnp.float32),
            pltpu.VMEM((5, SUB_STEP, count), jnp.float32),
            pltpu.VMEM((128, count), jnp.float32),
            pltpu.VMEM((2 * width, width), jnp.float32),
            pltpu.VMEM((n, depth, width), jnp.float32),
            pltpu.VMEM((2 * width, width), jnp.float32),
            pltpu.SemaphoreType.DMA((SLOTS,)),
            pltpu.SemaphoreType.DMA((SLOTS,)),
            pltpu.SemaphoreType.DMA((SLOTS,)),
            pltpu.SemaphoreType.DMA((SLOTS,)),
            pltpu.SemaphoreType.DMA,
            pltpu.SemaphoreType.DMA,
            pltpu.SemaphoreType.DMA((n,)),
            pltpu.SemaphoreType.DMA((n,)),
            pltpu.SemaphoreType.DMA((n,)),
            pltpu.SemaphoreType.DMA((n,)),
        ],
        compiler_params=pltpu.CompilerParams(
            collective_id=0, has_side_effects=True, vmem_limit_bytes=48 * 1024 * 1024),
        cost_estimate=pl.CostEstimate(
            flops=SLOTS * 2 * count * count * (width + 9), bytes_accessed=4 * count * width,
            transcendentals=SLOTS * count * count),
        name="panels",
    )(directions, geom)
    return product, gram if reduce_here else lax.psum(gram, "blk")


def solution(mesh):
    in_specs = (P("blk", "rhs"), P("blk"), P("blk"), P("blk"))
    out_specs = (P("blk", "rhs"), P(None, "rhs"))
    body = functools.partial(shards, mesh.shape["blk"])
    return jax.shard_map(body, mesh=mesh, in_specs=in_specs, out_specs=out_specs, check_vma=False)
```

```python
import functools

import jax
import jax.numpy as jnp
from jax import lax
from jax.experimental import pallas as pl
from jax.experimental.pallas import tpu as pltpu
from jax.sharding import PartitionSpec as P

MESH = pl.DeviceIdType.MESH
COL_STEP = 256
COL_GROUP = 1024
MIDDLE = 4.0
SOFTEN = 0.01
PIECES = 16
SLOTS = 7


def split_three(value):
    high = value.astype(jnp.bfloat16).astype(jnp.float32)
    rest = value - high
    mid = rest.astype(jnp.bfloat16).astype(jnp.float32)
    return high, mid, rest - mid


def panel_kernel(
    n, reduce_here, dirs_ref, geom_ref, product_ref, gram_ref,
    dirs, other, pieces, rows, flat, partial, landed, summed,
    send_dirs, recv_dirs, send_geom, recv_geom, send_other, recv_other,
    send_part, recv_part, send_sum, recv_sum,
):
    me = lax.axis_index("blk")
    half = lax.axis_index("rhs")
    count = dirs_ref.shape[0]
    width = dirs_ref.shape[1]
    sign = 1 - 2 * lax.rem(me, 2)

    def block(offset):
        return lax.rem(me + offset * sign + n, n)

    pair = block(1)

    barrier = pltpu.get_barrier_semaphore()
    pl.semaphore_signal(barrier, inc=1, device_id=(me, 1 - half), device_id_type=MESH)
    if reduce_here:
        def greet(step, carry):
            pl.semaphore_signal(barrier, inc=1, device_id=(lax.rem(me + step, n), half), device_id_type=MESH)
            return carry

        lax.fori_loop(1, n, greet, 0)
        pl.semaphore_wait(barrier, n)
    else:
        for offset in (1, -1, 2, -2, 3, -3):
            pl.semaphore_signal(barrier, inc=1, device_id=(block(offset), half), device_id_type=MESH)
        pl.semaphore_wait(barrier, 7)

    targets = ((1, pair), (2, block(-1)), (3, block(2)), (6, block(-3)))

    def dirs_copy(source, slot, target):
        return pltpu.make_async_remote_copy(
            src_ref=source, dst_ref=dirs.at[slot], send_sem=send_dirs.at[slot], recv_sem=recv_dirs.at[slot],
            device_id=(target, half), device_id_type=MESH)

    def geom_copy(source, slot, target):
        return pltpu.make_async_remote_copy(
            src_ref=source, dst_ref=pieces.at[slot], send_sem=send_geom.at[slot], recv_sem=recv_geom.at[slot],
            device_id=(target, half), device_id_type=MESH)

    for slot, target in targets:
        dirs_copy(dirs_ref, slot, target).start()
    across = pltpu.make_async_remote_copy(
        src_ref=dirs_ref, dst_ref=other, send_sem=send_other, recv_sem=recv_other,
        device_id=(me, 1 - half), device_id_type=MESH)
    across.start()

    axial = geom_ref[0:1, :] - MIDDLE
    cosine = geom_ref[1:2, :]
    sine = geom_ref[2:3, :]
    weight = geom_ref[3:4, :]
    scale = 1.0 / (weight * weight)
    norm = axial * axial + cosine * cosine + sine * sine + 0.5 * SOFTEN
    col_parts = (scale, norm * scale, axial * scale, cosine * scale, sine * scale)
    row_scale = scale * float(count)
    row_parts = (norm * row_scale, row_scale, -2.0 * axial * row_scale, -2.0 * cosine * row_scale,
                 -2.0 * sine * row_scale)
    flat[...] = jnp.zeros_like(flat)
    for at, part in enumerate(col_parts):
        for level, piece in enumerate(split_three(part)):
            flat[3 * at + level:3 * at + level + 1, :] = piece
    pieces[0] = flat[0:PIECES, :].astype(jnp.bfloat16)
    for slot, target in targets:
        geom_copy(pieces.at[0], slot, target).start()
    dirs[0] = dirs_ref[...]

    flat[...] = jnp.zeros_like(flat)
    for at, part in enumerate(row_parts):
        for level, piece in enumerate(split_three(part)):
            for spot in range(3):
                place = PIECES * level + 3 * at + spot
                flat[place:place + 1, :] = piece
    for start in range(0, count, 128):
        turned = flat[:, start:start + 128].T
        rows[start:start + 128, :] = turned[:, :3 * PIECES].astype(jnp.bfloat16)
    product_ref[...] = jnp.zeros_like(product_ref)

    def tile(slot):
        def step(at, carry):
            base = at * COL_GROUP
            row_feature = rows[...]

            def here(start):
                return pl.ds(pl.multiple_of(base + start, COL_STEP), COL_STEP)

            def squares(start):
                part = pieces[slot, :, here(start)]
                col_feature = jnp.concatenate([part, part, part], axis=0)
                return jnp.dot(row_feature, col_feature, preferred_element_type=jnp.float32)

            total = product_ref[...]
            square = squares(0)
            for start in range(0, COL_GROUP, COL_STEP):
                ahead = squares(start + COL_STEP) if start + COL_STEP < COL_GROUP else None
                values = lax.rsqrt(square).astype(jnp.bfloat16)
                total = total + jnp.dot(
                    values, dirs[slot, here(start), :], preferred_element_type=jnp.float32)
                square = ahead
            product_ref[...] = total
            return carry

        lax.fori_loop(0, count // COL_GROUP, step, 0)

    def turn(slot, carry):
        @pl.when(slot > 0)
        def _():
            dirs_copy(dirs_ref, slot, pair).wait_recv()
            geom_copy(pieces.at[0], slot, pair).wait_recv()

        @pl.when((slot == 2) | (slot == 3))
        def _():
            dirs_copy(dirs.at[slot], slot + 2, pair).start()
            geom_copy(pieces.at[slot], slot + 2, pair).start()

        tile(slot)
        return carry

    lax.fori_loop(0, SLOTS, turn, 0)

    across.wait()
    total = product_ref[...]
    high = total.astype(jnp.bfloat16)
    low = (total - high.astype(jnp.float32)).astype(jnp.bfloat16)
    inverse = 1.0 / (count * n)
    for place, value in ((half, dirs[0]), (1 - half, other[...])):
        turned = value.T
        inner = jnp.dot(turned, high, preferred_element_type=jnp.float32)
        inner = inner + jnp.dot(turned, low, preferred_element_type=jnp.float32)
        partial[pl.ds(pl.multiple_of(place * width, width), width), :] = inner * inverse

    if reduce_here:
        depth = landed.shape[1]

        def rows_of(owner):
            return pl.ds(pl.multiple_of(owner * depth, depth), depth)

        def part_copy(step):
            target = lax.rem(me + step, n)
            return pltpu.make_async_remote_copy(
                src_ref=partial.at[rows_of(target)], dst_ref=landed.at[step],
                send_sem=send_part.at[step], recv_sem=recv_part.at[step],
                device_id=(target, half), device_id_type=MESH)

        def sum_copy(step):
            target = lax.rem(me + step, n)
            return pltpu.make_async_remote_copy(
                src_ref=summed.at[rows_of(me)], dst_ref=summed.at[rows_of(me)],
                send_sem=send_sum.at[step], recv_sem=recv_sum.at[step],
                device_id=(target, half), device_id_type=MESH)

        def each(act):
            def run(step, carry):
                act(step)
                return carry

            lax.fori_loop(1, n, run, 0)

        each(lambda step: part_copy(step).start())
        landed[0] = partial[rows_of(me), :]
        each(lambda step: part_copy(step).wait_recv())
        summed[rows_of(me), :] = jnp.sum(landed[...], axis=0)
        each(lambda step: sum_copy(step).start())
        each(lambda step: sum_copy(step).wait_recv())
        gram_ref[...] = summed[...]
        each(lambda step: part_copy(step).wait_send())
        each(lambda step: sum_copy(step).wait_send())
    else:
        gram_ref[...] = partial[...]

    for slot in range(1, SLOTS):
        dirs_copy(dirs_ref, slot, pair).wait_send()
        geom_copy(pieces.at[0], slot, pair).wait_send()


def shards(n, directions, axial_pos, azimuth, panel_area):
    count, width = directions.shape
    angle = azimuth.astype(jnp.float32)
    geom = jnp.stack([axial_pos.astype(jnp.float32), jnp.cos(angle), jnp.sin(angle), panel_area.astype(jnp.float32)])
    vmem = pl.BlockSpec(memory_space=pltpu.VMEM)
    reduce_here = (2 * width) % (8 * n) == 0
    depth = 2 * width // n if reduce_here else 8
    product, gram = pl.pallas_call(
        functools.partial(panel_kernel, n, reduce_here),
        out_shape=(
            jax.ShapeDtypeStruct((count, width), jnp.float32),
            jax.ShapeDtypeStruct((2 * width, width), jnp.float32),
        ),
        in_specs=[vmem, vmem],
        out_specs=(vmem, vmem),
        scratch_shapes=[
            pltpu.VMEM((SLOTS, count, width), jnp.bfloat16),
            pltpu.VMEM((count, width), jnp.bfloat16),
            pltpu.VMEM((SLOTS, PIECES, count), jnp.bfloat16),
            pltpu.VMEM((count, 3 * PIECES), jnp.bfloat16),
            pltpu.VMEM((128, count), jnp.float32),
            pltpu.VMEM((2 * width, width), jnp.float32),
            pltpu.VMEM((n, depth, width), jnp.float32),
            pltpu.VMEM((2 * width, width), jnp.float32),
            pltpu.SemaphoreType.DMA((SLOTS,)),
            pltpu.SemaphoreType.DMA((SLOTS,)),
            pltpu.SemaphoreType.DMA((SLOTS,)),
            pltpu.SemaphoreType.DMA((SLOTS,)),
            pltpu.SemaphoreType.DMA,
            pltpu.SemaphoreType.DMA,
            pltpu.SemaphoreType.DMA((n,)),
            pltpu.SemaphoreType.DMA((n,)),
            pltpu.SemaphoreType.DMA((n,)),
            pltpu.SemaphoreType.DMA((n,)),
        ],
        compiler_params=pltpu.CompilerParams(
            collective_id=0, has_side_effects=True, vmem_limit_bytes=48 * 1024 * 1024),
        cost_estimate=pl.CostEstimate(
            flops=SLOTS * 2 * count * count * (width + 48), bytes_accessed=4 * count * width,
            transcendentals=SLOTS * count * count),
        name="panels",
    )(directions, geom)
    return product, gram if reduce_here else lax.psum(gram, "blk")


def solution(mesh):
    in_specs = (P("blk", "rhs"), P("blk"), P("blk"), P("blk"))
    out_specs = (P("blk", "rhs"), P(None, "rhs"))
    body = functools.partial(shards, mesh.shape["blk"])
    return jax.shard_map(body, mesh=mesh, in_specs=in_specs, out_specs=out_specs, check_vma=False)
```

```python
import functools

import jax
import jax.numpy as jnp
from jax import lax
from jax.experimental import pallas as pl
from jax.experimental.pallas import tpu as pltpu
from jax.sharding import PartitionSpec as P

MESH = pl.DeviceIdType.MESH
COL_STEP = 256
COL_GROUP = 1024
MIDDLE = 4.0
SOFTEN = 0.01
PIECES = 16
SLOTS = 7


def split_three(value):
    high = value.astype(jnp.bfloat16).astype(jnp.float32)
    rest = value - high
    mid = rest.astype(jnp.bfloat16).astype(jnp.float32)
    return high, mid, rest - mid


def panel_kernel(
    n, reduce_here, dirs_ref, geom_ref, product_ref, gram_ref,
    dirs, other, pieces, rows, flat, partial, landed, summed,
    send_dirs, recv_dirs, send_geom, recv_geom, send_other, recv_other,
    send_part, recv_part, send_sum, recv_sum,
):
    me = lax.axis_index("blk")
    half = lax.axis_index("rhs")
    count = dirs_ref.shape[0]
    width = dirs_ref.shape[1]
    sign = 1 - 2 * lax.rem(me, 2)

    def block(offset):
        return lax.rem(me + offset * sign + n, n)

    pair = block(1)

    barrier = pltpu.get_barrier_semaphore()
    pl.semaphore_signal(barrier, inc=1, device_id=(me, 1 - half), device_id_type=MESH)
    if reduce_here:
        def greet(step, carry):
            pl.semaphore_signal(barrier, inc=1, device_id=(lax.rem(me + step, n), half), device_id_type=MESH)
            return carry

        lax.fori_loop(1, n, greet, 0)
    else:
        for offset in (1, -1, 2, -2, 3, -3):
            pl.semaphore_signal(barrier, inc=1, device_id=(block(offset), half), device_id_type=MESH)

    targets = ((1, pair), (2, block(-1)), (3, block(2)), (6, block(-3)))

    def dirs_copy(source, slot, target):
        return pltpu.make_async_remote_copy(
            src_ref=source, dst_ref=dirs.at[slot], send_sem=send_dirs.at[slot], recv_sem=recv_dirs.at[slot],
            device_id=(target, half), device_id_type=MESH)

    def geom_copy(source, slot, target):
        return pltpu.make_async_remote_copy(
            src_ref=source, dst_ref=pieces.at[slot], send_sem=send_geom.at[slot], recv_sem=recv_geom.at[slot],
            device_id=(target, half), device_id_type=MESH)

    axial = geom_ref[0:1, :] - MIDDLE
    cosine = geom_ref[1:2, :]
    sine = geom_ref[2:3, :]
    weight = geom_ref[3:4, :]
    scale = 1.0 / (weight * weight)
    norm = axial * axial + cosine * cosine + sine * sine + 0.5 * SOFTEN
    col_parts = (scale, norm * scale, axial * scale, cosine * scale, sine * scale)
    row_scale = scale * float(count)
    row_parts = (norm * row_scale, row_scale, -2.0 * axial * row_scale, -2.0 * cosine * row_scale,
                 -2.0 * sine * row_scale)
    flat[...] = jnp.zeros_like(flat)
    for at, part in enumerate(col_parts):
        for level, piece in enumerate(split_three(part)):
            flat[3 * at + level:3 * at + level + 1, :] = piece
    pieces[0] = flat[0:PIECES, :].astype(jnp.bfloat16)
    pl.semaphore_wait(barrier, n if reduce_here else 7)
    for slot, target in targets:
        geom_copy(pieces.at[0], slot, target).start()
    for slot, target in targets:
        dirs_copy(dirs_ref, slot, target).start()
    across = pltpu.make_async_remote_copy(
        src_ref=dirs_ref, dst_ref=other, send_sem=send_other, recv_sem=recv_other,
        device_id=(me, 1 - half), device_id_type=MESH)
    across.start()

    dirs[0] = dirs_ref[...]

    flat[...] = jnp.zeros_like(flat)
    for at, part in enumerate(row_parts):
        for level, piece in enumerate(split_three(part)):
            for spot in range(3):
                place = PIECES * level + 3 * at + spot
                flat[place:place + 1, :] = piece
    for start in range(0, count, 128):
        turned = flat[:, start:start + 128].T
        rows[start:start + 128, :] = turned[:, :3 * PIECES].astype(jnp.bfloat16)
    product_ref[...] = jnp.zeros_like(product_ref)

    def tile(slot):
        def step(at, carry):
            base = at * COL_GROUP
            row_feature = rows[...]

            def here(start):
                return pl.ds(pl.multiple_of(base + start, COL_STEP), COL_STEP)

            def squares(start):
                part = pieces[slot, :, here(start)]
                col_feature = jnp.concatenate([part, part, part], axis=0)
                return jnp.dot(row_feature, col_feature, preferred_element_type=jnp.float32)

            total = product_ref[...]
            square = squares(0)
            for start in range(0, COL_GROUP, COL_STEP):
                ahead = squares(start + COL_STEP) if start + COL_STEP < COL_GROUP else None
                values = lax.rsqrt(square).astype(jnp.bfloat16)
                total = total + jnp.dot(
                    values, dirs[slot, here(start), :], preferred_element_type=jnp.float32)
                square = ahead
            product_ref[...] = total
            return carry

        lax.fori_loop(0, count // COL_GROUP, step, 0)

    def turn(slot, carry):
        @pl.when(slot > 0)
        def _():
            dirs_copy(dirs_ref, slot, pair).wait_recv()
            geom_copy(pieces.at[0], slot, pair).wait_recv()

        @pl.when((slot == 2) | (slot == 3))
        def _():
            dirs_copy(dirs.at[slot], slot + 2, pair).start()
            geom_copy(pieces.at[slot], slot + 2, pair).start()

        tile(slot)
        return carry

    lax.fori_loop(0, SLOTS, turn, 0)

    across.wait()
    total = product_ref[...]
    high = total.astype(jnp.bfloat16)
    low = (total - high.astype(jnp.float32)).astype(jnp.bfloat16)
    inverse = 1.0 / (count * n)
    for place, value in ((half, dirs[0]), (1 - half, other[...])):
        turned = value.T
        inner = jnp.dot(turned, high, preferred_element_type=jnp.float32)
        inner = inner + jnp.dot(turned, low, preferred_element_type=jnp.float32)
        partial[pl.ds(pl.multiple_of(place * width, width), width), :] = inner * inverse

    if reduce_here:
        depth = landed.shape[1]

        def rows_of(owner):
            return pl.ds(pl.multiple_of(owner * depth, depth), depth)

        def part_copy(step):
            target = lax.rem(me + step, n)
            return pltpu.make_async_remote_copy(
                src_ref=partial.at[rows_of(target)], dst_ref=landed.at[step],
                send_sem=send_part.at[step], recv_sem=recv_part.at[step],
                device_id=(target, half), device_id_type=MESH)

        def sum_copy(step):
            target = lax.rem(me + step, n)
            return pltpu.make_async_remote_copy(
                src_ref=summed.at[rows_of(me)], dst_ref=summed.at[rows_of(me)],
                send_sem=send_sum.at[step], recv_sem=recv_sum.at[step],
                device_id=(target, half), device_id_type=MESH)

        def each(act):
            def run(step, carry):
                act(step)
                return carry

            lax.fori_loop(1, n, run, 0)

        each(lambda step: part_copy(step).start())
        landed[0] = partial[rows_of(me), :]
        each(lambda step: part_copy(step).wait_recv())
        summed[rows_of(me), :] = jnp.sum(landed[...], axis=0)
        each(lambda step: sum_copy(step).start())
        each(lambda step: sum_copy(step).wait_recv())
        gram_ref[...] = summed[...]
        each(lambda step: part_copy(step).wait_send())
        each(lambda step: sum_copy(step).wait_send())
    else:
        gram_ref[...] = partial[...]

    for slot in range(1, SLOTS):
        dirs_copy(dirs_ref, slot, pair).wait_send()
        geom_copy(pieces.at[0], slot, pair).wait_send()


def shards(n, directions, axial_pos, azimuth, panel_area):
    count, width = directions.shape
    angle = azimuth.astype(jnp.float32)
    geom = jnp.stack([axial_pos.astype(jnp.float32), jnp.cos(angle), jnp.sin(angle), panel_area.astype(jnp.float32)])
    vmem = pl.BlockSpec(memory_space=pltpu.VMEM)
    reduce_here = (2 * width) % (8 * n) == 0
    depth = 2 * width // n if reduce_here else 8
    product, gram = pl.pallas_call(
        functools.partial(panel_kernel, n, reduce_here),
        out_shape=(
            jax.ShapeDtypeStruct((count, width), jnp.float32),
            jax.ShapeDtypeStruct((2 * width, width), jnp.float32),
        ),
        in_specs=[vmem, vmem],
        out_specs=(vmem, vmem),
        scratch_shapes=[
            pltpu.VMEM((SLOTS, count, width), jnp.bfloat16),
            pltpu.VMEM((count, width), jnp.bfloat16),
            pltpu.VMEM((SLOTS, PIECES, count), jnp.bfloat16),
            pltpu.VMEM((count, 3 * PIECES), jnp.bfloat16),
            pltpu.VMEM((128, count), jnp.float32),
            pltpu.VMEM((2 * width, width), jnp.float32),
            pltpu.VMEM((n, depth, width), jnp.float32),
            pltpu.VMEM((2 * width, width), jnp.float32),
            pltpu.SemaphoreType.DMA((SLOTS,)),
            pltpu.SemaphoreType.DMA((SLOTS,)),
            pltpu.SemaphoreType.DMA((SLOTS,)),
            pltpu.SemaphoreType.DMA((SLOTS,)),
            pltpu.SemaphoreType.DMA,
            pltpu.SemaphoreType.DMA,
            pltpu.SemaphoreType.DMA((n,)),
            pltpu.SemaphoreType.DMA((n,)),
            pltpu.SemaphoreType.DMA((n,)),
            pltpu.SemaphoreType.DMA((n,)),
        ],
        compiler_params=pltpu.CompilerParams(
            collective_id=0, has_side_effects=True, vmem_limit_bytes=48 * 1024 * 1024),
        cost_estimate=pl.CostEstimate(
            flops=SLOTS * 2 * count * count * (width + 48), bytes_accessed=4 * count * width,
            transcendentals=SLOTS * count * count),
        name="panels",
    )(directions, geom)
    return product, gram if reduce_here else lax.psum(gram, "blk")


def solution(mesh):
    in_specs = (P("blk", "rhs"), P("blk"), P("blk"), P("blk"))
    out_specs = (P("blk", "rhs"), P(None, "rhs"))
    body = functools.partial(shards, mesh.shape["blk"])
    return jax.shard_map(body, mesh=mesh, in_specs=in_specs, out_specs=out_specs, check_vma=False)
```

```python
import functools

import jax
import jax.numpy as jnp
from jax import lax
from jax.experimental import pallas as pl
from jax.experimental.pallas import tpu as pltpu
from jax.sharding import PartitionSpec as P

MESH = pl.DeviceIdType.MESH
COL_STEP = 512
ROW_STEP = 512
MIDDLE = 4.0
SOFTEN = 0.01
PIECES = 16
SLOTS = 7


def split_three(value):
    high = value.astype(jnp.bfloat16).astype(jnp.float32)
    rest = value - high
    mid = rest.astype(jnp.bfloat16).astype(jnp.float32)
    return high, mid, rest - mid


def panel_kernel(
    n, reduce_here, dirs_ref, geom_ref, product_ref, gram_ref,
    dirs, other, pieces, rows, turned_product, flat, partial, landed, summed,
    send_dirs, recv_dirs, send_geom, recv_geom, send_other, recv_other,
    send_part, recv_part, send_sum, recv_sum,
):
    me = lax.axis_index("blk")
    half = lax.axis_index("rhs")
    count = dirs_ref.shape[0]
    width = dirs_ref.shape[1]
    sign = 1 - 2 * lax.rem(me, 2)

    def block(offset):
        return lax.rem(me + offset * sign + n, n)

    pair = block(1)

    barrier = pltpu.get_barrier_semaphore()
    pl.semaphore_signal(barrier, inc=1, device_id=(me, 1 - half), device_id_type=MESH)
    if reduce_here:
        def greet(step, carry):
            pl.semaphore_signal(barrier, inc=1, device_id=(lax.rem(me + step, n), half), device_id_type=MESH)
            return carry

        lax.fori_loop(1, n, greet, 0)
    else:
        for offset in (1, -1, 2, -2, 3, -3):
            pl.semaphore_signal(barrier, inc=1, device_id=(block(offset), half), device_id_type=MESH)

    targets = ((1, pair), (2, block(-1)), (3, block(2)), (6, block(-3)))

    def dirs_copy(source, slot, target):
        return pltpu.make_async_remote_copy(
            src_ref=source, dst_ref=dirs.at[slot], send_sem=send_dirs.at[slot], recv_sem=recv_dirs.at[slot],
            device_id=(target, half), device_id_type=MESH)

    def geom_copy(source, slot, target):
        return pltpu.make_async_remote_copy(
            src_ref=source, dst_ref=pieces.at[slot], send_sem=send_geom.at[slot], recv_sem=recv_geom.at[slot],
            device_id=(target, half), device_id_type=MESH)

    axial = geom_ref[0:1, :] - MIDDLE
    cosine = geom_ref[1:2, :]
    sine = geom_ref[2:3, :]
    weight = geom_ref[3:4, :]
    scale = 1.0 / (weight * weight)
    norm = axial * axial + cosine * cosine + sine * sine + 0.5 * SOFTEN
    col_parts = (scale, norm * scale, axial * scale, cosine * scale, sine * scale)
    row_scale = scale * float(count)
    row_parts = (norm * row_scale, row_scale, -2.0 * axial * row_scale, -2.0 * cosine * row_scale,
                 -2.0 * sine * row_scale)
    flat[...] = jnp.zeros_like(flat)
    for at, part in enumerate(col_parts):
        for level, piece in enumerate(split_three(part)):
            flat[3 * at + level:3 * at + level + 1, :] = piece
    pieces[0] = flat[0:PIECES, :].astype(jnp.bfloat16)
    pl.semaphore_wait(barrier, n if reduce_here else 7)
    for slot, target in targets:
        geom_copy(pieces.at[0], slot, target).start()
    for start in range(0, count, 128):
        strip = dirs_ref[start:start + 128, :].astype(jnp.float32)
        dirs[0, :, start:start + 128] = strip.T.astype(jnp.bfloat16)
    for slot, target in targets:
        dirs_copy(dirs.at[0], slot, target).start()
    across = pltpu.make_async_remote_copy(
        src_ref=dirs.at[0], dst_ref=other, send_sem=send_other, recv_sem=recv_other,
        device_id=(me, 1 - half), device_id_type=MESH)
    across.start()

    flat[...] = jnp.zeros_like(flat)
    for at, part in enumerate(row_parts):
        for level, piece in enumerate(split_three(part)):
            for spot in range(3):
                place = PIECES * level + 3 * at + spot
                flat[place:place + 1, :] = piece
    rows[...] = flat[0:3 * PIECES, :].astype(jnp.bfloat16)
    turned_product[...] = jnp.zeros_like(turned_product)

    def tile(slot):
        def step(at, carry):
            here = pl.ds(pl.multiple_of(at * COL_STEP, COL_STEP), COL_STEP)
            part = pieces[slot, :, here].astype(jnp.float32)
            col_feature = jnp.concatenate([part, part, part], axis=0).T.astype(jnp.bfloat16)
            block_dirs = dirs[slot, :, here]

            def squares(start):
                return jnp.dot(col_feature, rows[:, start:start + ROW_STEP], preferred_element_type=jnp.float32)

            square = squares(0)
            for start in range(0, count, ROW_STEP):
                ahead = squares(start + ROW_STEP) if start + ROW_STEP < count else None
                values = lax.rsqrt(square).astype(jnp.bfloat16)
                turned_product[:, start:start + ROW_STEP] += jnp.dot(
                    block_dirs, values, preferred_element_type=jnp.float32)
                square = ahead
            return carry

        lax.fori_loop(0, count // COL_STEP, step, 0)

    def turn(slot, carry):
        @pl.when(slot > 0)
        def _():
            dirs_copy(dirs.at[0], slot, pair).wait_recv()
            geom_copy(pieces.at[0], slot, pair).wait_recv()

        @pl.when((slot == 2) | (slot == 3))
        def _():
            dirs_copy(dirs.at[slot], slot + 2, pair).start()
            geom_copy(pieces.at[slot], slot + 2, pair).start()

        tile(slot)
        return carry

    lax.fori_loop(0, SLOTS, turn, 0)

    across.wait()
    for start in range(0, count, 128):
        product_ref[start:start + 128, :] = turned_product[:, start:start + 128].T
    total = product_ref[...]
    high = total.astype(jnp.bfloat16)
    low = (total - high.astype(jnp.float32)).astype(jnp.bfloat16)
    inverse = 1.0 / (count * n)
    for place, value in ((half, dirs[0]), (1 - half, other[...])):
        inner = jnp.dot(value, high, preferred_element_type=jnp.float32)
        inner = inner + jnp.dot(value, low, preferred_element_type=jnp.float32)
        partial[pl.ds(pl.multiple_of(place * width, width), width), :] = inner * inverse

    if reduce_here:
        depth = landed.shape[1]

        def rows_of(owner):
            return pl.ds(pl.multiple_of(owner * depth, depth), depth)

        def part_copy(step):
            target = lax.rem(me + step, n)
            return pltpu.make_async_remote_copy(
                src_ref=partial.at[rows_of(target)], dst_ref=landed.at[step],
                send_sem=send_part.at[step], recv_sem=recv_part.at[step],
                device_id=(target, half), device_id_type=MESH)

        def sum_copy(step):
            target = lax.rem(me + step, n)
            return pltpu.make_async_remote_copy(
                src_ref=summed.at[rows_of(me)], dst_ref=summed.at[rows_of(me)],
                send_sem=send_sum.at[step], recv_sem=recv_sum.at[step],
                device_id=(target, half), device_id_type=MESH)

        def each(act):
            def run(step, carry):
                act(step)
                return carry

            lax.fori_loop(1, n, run, 0)

        each(lambda step: part_copy(step).start())
        landed[0] = partial[rows_of(me), :]
        each(lambda step: part_copy(step).wait_recv())
        summed[rows_of(me), :] = jnp.sum(landed[...], axis=0)
        each(lambda step: sum_copy(step).start())
        each(lambda step: sum_copy(step).wait_recv())
        gram_ref[...] = summed[...]
        each(lambda step: part_copy(step).wait_send())
        each(lambda step: sum_copy(step).wait_send())
    else:
        gram_ref[...] = partial[...]

    for slot in range(1, SLOTS):
        dirs_copy(dirs.at[0], slot, pair).wait_send()
        geom_copy(pieces.at[0], slot, pair).wait_send()


def shards(n, directions, axial_pos, azimuth, panel_area):
    count, width = directions.shape
    angle = azimuth.astype(jnp.float32)
    geom = jnp.stack([axial_pos.astype(jnp.float32), jnp.cos(angle), jnp.sin(angle), panel_area.astype(jnp.float32)])
    vmem = pl.BlockSpec(memory_space=pltpu.VMEM)
    reduce_here = (2 * width) % (8 * n) == 0
    depth = 2 * width // n if reduce_here else 8
    product, gram = pl.pallas_call(
        functools.partial(panel_kernel, n, reduce_here),
        out_shape=(
            jax.ShapeDtypeStruct((count, width), jnp.float32),
            jax.ShapeDtypeStruct((2 * width, width), jnp.float32),
        ),
        in_specs=[vmem, vmem],
        out_specs=(vmem, vmem),
        scratch_shapes=[
            pltpu.VMEM((SLOTS, width, count), jnp.bfloat16),
            pltpu.VMEM((width, count), jnp.bfloat16),
            pltpu.VMEM((SLOTS, PIECES, count), jnp.bfloat16),
            pltpu.VMEM((3 * PIECES, count), jnp.bfloat16),
            pltpu.VMEM((width, count), jnp.float32),
            pltpu.VMEM((128, count), jnp.float32),
            pltpu.VMEM((2 * width, width), jnp.float32),
            pltpu.VMEM((n, depth, width), jnp.float32),
            pltpu.VMEM((2 * width, width), jnp.float32),
            pltpu.SemaphoreType.DMA((SLOTS,)),
            pltpu.SemaphoreType.DMA((SLOTS,)),
            pltpu.SemaphoreType.DMA((SLOTS,)),
            pltpu.SemaphoreType.DMA((SLOTS,)),
            pltpu.SemaphoreType.DMA,
            pltpu.SemaphoreType.DMA,
            pltpu.SemaphoreType.DMA((n,)),
            pltpu.SemaphoreType.DMA((n,)),
            pltpu.SemaphoreType.DMA((n,)),
            pltpu.SemaphoreType.DMA((n,)),
        ],
        compiler_params=pltpu.CompilerParams(
            collective_id=0, has_side_effects=True, vmem_limit_bytes=48 * 1024 * 1024),
        cost_estimate=pl.CostEstimate(
            flops=SLOTS * 2 * count * count * (width + 48), bytes_accessed=4 * count * width,
            transcendentals=SLOTS * count * count),
        name="panels",
    )(directions, geom)
    return product, gram if reduce_here else lax.psum(gram, "blk")


def solution(mesh):
    in_specs = (P("blk", "rhs"), P("blk"), P("blk"), P("blk"))
    out_specs = (P("blk", "rhs"), P(None, "rhs"))
    body = functools.partial(shards, mesh.shape["blk"])
    return jax.shard_map(body, mesh=mesh, in_specs=in_specs, out_specs=out_specs, check_vma=False)
```

```python
import functools

import jax
import jax.numpy as jnp
from jax import lax
from jax.experimental import pallas as pl
from jax.experimental.pallas import tpu as pltpu
from jax.sharding import PartitionSpec as P

MESH = pl.DeviceIdType.MESH
COL_STEP = 512
ROW_STEP = 512
CUT = 32
MIDDLE = 4.0
SOFTEN = 0.01
PIECES = 16
SLOTS = 7


def split_three(value):
    high = value.astype(jnp.bfloat16).astype(jnp.float32)
    rest = value - high
    mid = rest.astype(jnp.bfloat16).astype(jnp.float32)
    return high, mid, rest - mid


def panel_kernel(
    n, reduce_here, dirs_ref, geom_ref, product_ref, gram_ref,
    dirs, other, pieces, rows, turned_product, flat, partial, landed, summed,
    send_dirs, recv_dirs, send_geom, recv_geom, send_other, recv_other,
    send_part, recv_part, send_sum, recv_sum,
):
    me = lax.axis_index("blk")
    half = lax.axis_index("rhs")
    count = dirs_ref.shape[0]
    width = dirs_ref.shape[1]
    sign = 1 - 2 * lax.rem(me, 2)

    def block(offset):
        return lax.rem(me + offset * sign + n, n)

    pair = block(1)

    barrier = pltpu.get_barrier_semaphore()
    pl.semaphore_signal(barrier, inc=1, device_id=(me, 1 - half), device_id_type=MESH)
    if reduce_here:
        def greet(step, carry):
            pl.semaphore_signal(barrier, inc=1, device_id=(lax.rem(me + step, n), half), device_id_type=MESH)
            return carry

        lax.fori_loop(1, n, greet, 0)
    else:
        for offset in (1, -1, 2, -2, 3, -3):
            pl.semaphore_signal(barrier, inc=1, device_id=(block(offset), half), device_id_type=MESH)

    targets = ((1, pair), (2, block(-1)), (3, block(2)), (6, block(-3)))

    def dirs_copy(source, slot, target):
        return pltpu.make_async_remote_copy(
            src_ref=source, dst_ref=dirs.at[slot], send_sem=send_dirs.at[slot], recv_sem=recv_dirs.at[slot],
            device_id=(target, half), device_id_type=MESH)

    def geom_copy(source, slot, target):
        return pltpu.make_async_remote_copy(
            src_ref=source, dst_ref=pieces.at[slot], send_sem=send_geom.at[slot], recv_sem=recv_geom.at[slot],
            device_id=(target, half), device_id_type=MESH)

    axial = geom_ref[0:1, :] - MIDDLE
    cosine = geom_ref[1:2, :]
    sine = geom_ref[2:3, :]
    weight = geom_ref[3:4, :]
    scale = 1.0 / (weight * weight)
    norm = axial * axial + cosine * cosine + sine * sine + 0.5 * SOFTEN
    col_parts = (scale, norm * scale, axial * scale, cosine * scale, sine * scale)
    row_scale = scale * float(count)
    row_parts = (norm * row_scale, row_scale, -2.0 * axial * row_scale, -2.0 * cosine * row_scale,
                 -2.0 * sine * row_scale)
    flat[...] = jnp.zeros_like(flat)
    for at, part in enumerate(col_parts):
        for level, piece in enumerate(split_three(part)):
            flat[3 * at + level:3 * at + level + 1, :] = piece
    pieces[0] = flat[0:PIECES, :].astype(jnp.bfloat16)
    pl.semaphore_wait(barrier, n if reduce_here else 7)
    for slot, target in targets:
        geom_copy(pieces.at[0], slot, target).start()
    for start in range(0, count, 128):
        strip = dirs_ref[start:start + 128, :].astype(jnp.float32)
        dirs[0, :, start:start + 128] = strip.T.astype(jnp.bfloat16)
    def cut_copy(source, slot, target, first):
        return pltpu.make_async_remote_copy(
            src_ref=dirs.at[source, first:first + CUT], dst_ref=dirs.at[slot, first:first + CUT],
            send_sem=send_dirs.at[slot], recv_sem=recv_dirs.at[slot],
            device_id=(target, half), device_id_type=MESH)

    def across_copy(first, depth):
        return pltpu.make_async_remote_copy(
            src_ref=dirs.at[0, first:first + depth], dst_ref=other.at[first:first + depth],
            send_sem=send_other, recv_sem=recv_other,
            device_id=(me, 1 - half), device_id_type=MESH)

    for group in (targets[:1], targets[1:3], targets[3:]):
        for first in range(0, width, CUT):
            for slot, target in group:
                cut_copy(0, slot, target, first).start()
            if group[0][0] == 6:
                across_copy(first, CUT).start()
    across = across_copy(0, width)

    flat[...] = jnp.zeros_like(flat)
    for at, part in enumerate(row_parts):
        for level, piece in enumerate(split_three(part)):
            for spot in range(3):
                place = PIECES * level + 3 * at + spot
                flat[place:place + 1, :] = piece
    rows[...] = flat[0:3 * PIECES, :].astype(jnp.bfloat16)
    turned_product[...] = jnp.zeros_like(turned_product)

    def tile(slot):
        def step(at, carry):
            here = pl.ds(pl.multiple_of(at * COL_STEP, COL_STEP), COL_STEP)
            part = pieces[slot, :, here].astype(jnp.float32)
            col_feature = jnp.concatenate([part, part, part], axis=0).T.astype(jnp.bfloat16)
            block_dirs = dirs[slot, :, here]

            def squares(start):
                return jnp.dot(col_feature, rows[:, start:start + ROW_STEP], preferred_element_type=jnp.float32)

            square = squares(0)
            for start in range(0, count, ROW_STEP):
                ahead = squares(start + ROW_STEP) if start + ROW_STEP < count else None
                values = lax.rsqrt(square).astype(jnp.bfloat16)
                turned_product[:, start:start + ROW_STEP] += jnp.dot(
                    block_dirs, values, preferred_element_type=jnp.float32)
                square = ahead
            return carry

        lax.fori_loop(0, count // COL_STEP, step, 0)

    def turn(slot, carry):
        @pl.when(slot > 0)
        def _():
            dirs_copy(dirs.at[0], slot, pair).wait_recv()
            geom_copy(pieces.at[0], slot, pair).wait_recv()

        @pl.when((slot == 2) | (slot == 3))
        def _():
            for first in range(0, width, CUT):
                cut_copy(slot, slot + 2, pair, first).start()
            geom_copy(pieces.at[slot], slot + 2, pair).start()

        tile(slot)
        return carry

    lax.fori_loop(0, SLOTS, turn, 0)

    across.wait()
    for start in range(0, count, 128):
        product_ref[start:start + 128, :] = turned_product[:, start:start + 128].T
    total = product_ref[...]
    high = total.astype(jnp.bfloat16)
    low = (total - high.astype(jnp.float32)).astype(jnp.bfloat16)
    inverse = 1.0 / (count * n)
    for place, value in ((half, dirs[0]), (1 - half, other[...])):
        inner = jnp.dot(value, high, preferred_element_type=jnp.float32)
        inner = inner + jnp.dot(value, low, preferred_element_type=jnp.float32)
        partial[pl.ds(pl.multiple_of(place * width, width), width), :] = inner * inverse

    if reduce_here:
        depth = landed.shape[1]

        def rows_of(owner):
            return pl.ds(pl.multiple_of(owner * depth, depth), depth)

        def part_copy(step):
            target = lax.rem(me + step, n)
            return pltpu.make_async_remote_copy(
                src_ref=partial.at[rows_of(target)], dst_ref=landed.at[step],
                send_sem=send_part.at[step], recv_sem=recv_part.at[step],
                device_id=(target, half), device_id_type=MESH)

        def sum_copy(step):
            target = lax.rem(me + step, n)
            return pltpu.make_async_remote_copy(
                src_ref=summed.at[rows_of(me)], dst_ref=summed.at[rows_of(me)],
                send_sem=send_sum.at[step], recv_sem=recv_sum.at[step],
                device_id=(target, half), device_id_type=MESH)

        def each(act):
            def run(step, carry):
                act(step)
                return carry

            lax.fori_loop(1, n, run, 0)

        each(lambda step: part_copy(step).start())
        landed[0] = partial[rows_of(me), :]
        each(lambda step: part_copy(step).wait_recv())
        summed[rows_of(me), :] = jnp.sum(landed[...], axis=0)
        each(lambda step: sum_copy(step).start())
        each(lambda step: sum_copy(step).wait_recv())
        gram_ref[...] = summed[...]
        each(lambda step: part_copy(step).wait_send())
        each(lambda step: sum_copy(step).wait_send())
    else:
        gram_ref[...] = partial[...]

    for slot in range(1, SLOTS):
        dirs_copy(dirs.at[0], slot, pair).wait_send()
        geom_copy(pieces.at[0], slot, pair).wait_send()


def shards(n, directions, axial_pos, azimuth, panel_area):
    count, width = directions.shape
    angle = azimuth.astype(jnp.float32)
    geom = jnp.stack([axial_pos.astype(jnp.float32), jnp.cos(angle), jnp.sin(angle), panel_area.astype(jnp.float32)])
    vmem = pl.BlockSpec(memory_space=pltpu.VMEM)
    reduce_here = (2 * width) % (8 * n) == 0
    depth = 2 * width // n if reduce_here else 8
    product, gram = pl.pallas_call(
        functools.partial(panel_kernel, n, reduce_here),
        out_shape=(
            jax.ShapeDtypeStruct((count, width), jnp.float32),
            jax.ShapeDtypeStruct((2 * width, width), jnp.float32),
        ),
        in_specs=[vmem, vmem],
        out_specs=(vmem, vmem),
        scratch_shapes=[
            pltpu.VMEM((SLOTS, width, count), jnp.bfloat16),
            pltpu.VMEM((width, count), jnp.bfloat16),
            pltpu.VMEM((SLOTS, PIECES, count), jnp.bfloat16),
            pltpu.VMEM((3 * PIECES, count), jnp.bfloat16),
            pltpu.VMEM((width, count), jnp.float32),
            pltpu.VMEM((128, count), jnp.float32),
            pltpu.VMEM((2 * width, width), jnp.float32),
            pltpu.VMEM((n, depth, width), jnp.float32),
            pltpu.VMEM((2 * width, width), jnp.float32),
            pltpu.SemaphoreType.DMA((SLOTS,)),
            pltpu.SemaphoreType.DMA((SLOTS,)),
            pltpu.SemaphoreType.DMA((SLOTS,)),
            pltpu.SemaphoreType.DMA((SLOTS,)),
            pltpu.SemaphoreType.DMA,
            pltpu.SemaphoreType.DMA,
            pltpu.SemaphoreType.DMA((n,)),
            pltpu.SemaphoreType.DMA((n,)),
            pltpu.SemaphoreType.DMA((n,)),
            pltpu.SemaphoreType.DMA((n,)),
        ],
        compiler_params=pltpu.CompilerParams(
            collective_id=0, has_side_effects=True, vmem_limit_bytes=48 * 1024 * 1024),
        cost_estimate=pl.CostEstimate(
            flops=SLOTS * 2 * count * count * (width + 48), bytes_accessed=4 * count * width,
            transcendentals=SLOTS * count * count),
        name="panels",
    )(directions, geom)
    return product, gram if reduce_here else lax.psum(gram, "blk")


def solution(mesh):
    in_specs = (P("blk", "rhs"), P("blk"), P("blk"), P("blk"))
    out_specs = (P("blk", "rhs"), P(None, "rhs"))
    body = functools.partial(shards, mesh.shape["blk"])
    return jax.shard_map(body, mesh=mesh, in_specs=in_specs, out_specs=out_specs, check_vma=False)
```

```python
import functools

import jax
import jax.numpy as jnp
from jax import lax
from jax.experimental import pallas as pl
from jax.experimental.pallas import tpu as pltpu
from jax.sharding import PartitionSpec as P

MESH = pl.DeviceIdType.MESH
COL_STEP = 512
ROW_STEP = 512
MIDDLE = 4.0
SOFTEN = 0.01
PIECES = 16
SLOTS = 7


def split_three(value):
    high = value.astype(jnp.bfloat16).astype(jnp.float32)
    rest = value - high
    mid = rest.astype(jnp.bfloat16).astype(jnp.float32)
    return high, mid, rest - mid


def panel_kernel(
    n, reduce_here, dirs_ref, geom_ref, product_ref, gram_ref,
    dirs, other, pieces, rows, turned_product, flat, partial, landed, summed,
    send_dirs, recv_dirs, send_geom, recv_geom, send_other, recv_other,
    send_part, recv_part, send_sum, recv_sum,
):
    me = lax.axis_index("blk")
    half = lax.axis_index("rhs")
    count = dirs_ref.shape[0]
    width = dirs_ref.shape[1]
    sign = 1 - 2 * lax.rem(me, 2)

    def block(offset):
        return lax.rem(me + offset * sign + n, n)

    pair = block(1)

    barrier = pltpu.get_barrier_semaphore()
    pl.semaphore_signal(barrier, inc=1, device_id=(me, 1 - half), device_id_type=MESH)
    if reduce_here:
        def greet(step, carry):
            pl.semaphore_signal(barrier, inc=1, device_id=(lax.rem(me + step, n), half), device_id_type=MESH)
            return carry

        lax.fori_loop(1, n, greet, 0)
    else:
        for offset in (1, -1, 2, -2, 3, -3):
            pl.semaphore_signal(barrier, inc=1, device_id=(block(offset), half), device_id_type=MESH)

    targets = ((1, pair), (2, block(-1)), (3, block(2)), (6, block(-3)))

    def dirs_copy(source, slot, target):
        return pltpu.make_async_remote_copy(
            src_ref=source, dst_ref=dirs.at[slot], send_sem=send_dirs.at[slot], recv_sem=recv_dirs.at[slot],
            device_id=(target, half), device_id_type=MESH)

    def geom_copy(source, slot, target):
        return pltpu.make_async_remote_copy(
            src_ref=source, dst_ref=pieces.at[slot], send_sem=send_geom.at[slot], recv_sem=recv_geom.at[slot],
            device_id=(target, half), device_id_type=MESH)

    axial = geom_ref[0:1, :] - MIDDLE
    cosine = geom_ref[1:2, :]
    sine = geom_ref[2:3, :]
    weight = geom_ref[3:4, :]
    scale = 1.0 / (weight * weight)
    norm = axial * axial + cosine * cosine + sine * sine + 0.5 * SOFTEN
    col_parts = (scale, norm * scale, axial * scale, cosine * scale, sine * scale)
    row_scale = scale * float(count)
    row_parts = (norm * row_scale, row_scale, -2.0 * axial * row_scale, -2.0 * cosine * row_scale,
                 -2.0 * sine * row_scale)
    flat[...] = jnp.zeros_like(flat)
    for at, part in enumerate(col_parts):
        for level, piece in enumerate(split_three(part)):
            flat[3 * at + level:3 * at + level + 1, :] = piece
    pieces[0] = flat[0:PIECES, :].astype(jnp.bfloat16)
    pl.semaphore_wait(barrier, n if reduce_here else 7)
    for slot, target in targets:
        geom_copy(pieces.at[0], slot, target).start()
    for start in range(0, count, 128):
        strip = dirs_ref[start:start + 128, :].astype(jnp.float32)
        dirs[0, :, start:start + 128] = strip.T.astype(jnp.bfloat16)
    for slot, target in targets:
        dirs_copy(dirs.at[0], slot, target).start()
    across = pltpu.make_async_remote_copy(
        src_ref=dirs.at[0], dst_ref=other, send_sem=send_other, recv_sem=recv_other,
        device_id=(me, 1 - half), device_id_type=MESH)
    across.start()

    flat[...] = jnp.zeros_like(flat)
    for at, part in enumerate(row_parts):
        for level, piece in enumerate(split_three(part)):
            for spot in range(3):
                place = PIECES * level + 3 * at + spot
                flat[place:place + 1, :] = piece
    rows[...] = flat[0:3 * PIECES, :].astype(jnp.bfloat16)
    turned_product[...] = jnp.zeros_like(turned_product)

    def tile(slot):
        def step(at, carry):
            here = pl.ds(pl.multiple_of(at * COL_STEP, COL_STEP), COL_STEP)
            part = pieces[slot, :, here].astype(jnp.float32)
            col_feature = jnp.concatenate([part, part, part], axis=0).T.astype(jnp.bfloat16)
            block_dirs = dirs[slot, :, here]

            def squares(start):
                return jnp.dot(col_feature, rows[:, start:start + ROW_STEP], preferred_element_type=jnp.float32)

            square = squares(0)
            for start in range(0, count, ROW_STEP):
                ahead = squares(start + ROW_STEP) if start + ROW_STEP < count else None
                values = lax.rsqrt(square.astype(jnp.bfloat16))
                turned_product[:, start:start + ROW_STEP] += jnp.dot(
                    block_dirs, values, preferred_element_type=jnp.float32)
                square = ahead
            return carry

        lax.fori_loop(0, count // COL_STEP, step, 0)

    def turn(slot, carry):
        @pl.when(slot > 0)
        def _():
            dirs_copy(dirs.at[0], slot, pair).wait_recv()
            geom_copy(pieces.at[0], slot, pair).wait_recv()

        @pl.when((slot == 2) | (slot == 3))
        def _():
            dirs_copy(dirs.at[slot], slot + 2, pair).start()
            geom_copy(pieces.at[slot], slot + 2, pair).start()

        tile(slot)
        return carry

    lax.fori_loop(0, SLOTS, turn, 0)

    across.wait()
    for start in range(0, count, 128):
        product_ref[start:start + 128, :] = turned_product[:, start:start + 128].T
    total = product_ref[...]
    high = total.astype(jnp.bfloat16)
    low = (total - high.astype(jnp.float32)).astype(jnp.bfloat16)
    inverse = 1.0 / (count * n)
    for place, value in ((half, dirs[0]), (1 - half, other[...])):
        inner = jnp.dot(value, high, preferred_element_type=jnp.float32)
        inner = inner + jnp.dot(value, low, preferred_element_type=jnp.float32)
        partial[pl.ds(pl.multiple_of(place * width, width), width), :] = inner * inverse

    if reduce_here:
        depth = landed.shape[1]

        def rows_of(owner):
            return pl.ds(pl.multiple_of(owner * depth, depth), depth)

        def part_copy(step):
            target = lax.rem(me + step, n)
            return pltpu.make_async_remote_copy(
                src_ref=partial.at[rows_of(target)], dst_ref=landed.at[step],
                send_sem=send_part.at[step], recv_sem=recv_part.at[step],
                device_id=(target, half), device_id_type=MESH)

        def sum_copy(step):
            target = lax.rem(me + step, n)
            return pltpu.make_async_remote_copy(
                src_ref=summed.at[rows_of(me)], dst_ref=summed.at[rows_of(me)],
                send_sem=send_sum.at[step], recv_sem=recv_sum.at[step],
                device_id=(target, half), device_id_type=MESH)

        def each(act):
            def run(step, carry):
                act(step)
                return carry

            lax.fori_loop(1, n, run, 0)

        each(lambda step: part_copy(step).start())
        landed[0] = partial[rows_of(me), :]
        each(lambda step: part_copy(step).wait_recv())
        summed[rows_of(me), :] = jnp.sum(landed[...], axis=0)
        each(lambda step: sum_copy(step).start())
        each(lambda step: sum_copy(step).wait_recv())
        gram_ref[...] = summed[...]
        each(lambda step: part_copy(step).wait_send())
        each(lambda step: sum_copy(step).wait_send())
    else:
        gram_ref[...] = partial[...]

    for slot in range(1, SLOTS):
        dirs_copy(dirs.at[0], slot, pair).wait_send()
        geom_copy(pieces.at[0], slot, pair).wait_send()


def shards(n, directions, axial_pos, azimuth, panel_area):
    count, width = directions.shape
    angle = azimuth.astype(jnp.float32)
    geom = jnp.stack([axial_pos.astype(jnp.float32), jnp.cos(angle), jnp.sin(angle), panel_area.astype(jnp.float32)])
    vmem = pl.BlockSpec(memory_space=pltpu.VMEM)
    reduce_here = (2 * width) % (8 * n) == 0
    depth = 2 * width // n if reduce_here else 8
    product, gram = pl.pallas_call(
        functools.partial(panel_kernel, n, reduce_here),
        out_shape=(
            jax.ShapeDtypeStruct((count, width), jnp.float32),
            jax.ShapeDtypeStruct((2 * width, width), jnp.float32),
        ),
        in_specs=[vmem, vmem],
        out_specs=(vmem, vmem),
        scratch_shapes=[
            pltpu.VMEM((SLOTS, width, count), jnp.bfloat16),
            pltpu.VMEM((width, count), jnp.bfloat16),
            pltpu.VMEM((SLOTS, PIECES, count), jnp.bfloat16),
            pltpu.VMEM((3 * PIECES, count), jnp.bfloat16),
            pltpu.VMEM((width, count), jnp.float32),
            pltpu.VMEM((128, count), jnp.float32),
            pltpu.VMEM((2 * width, width), jnp.float32),
            pltpu.VMEM((n, depth, width), jnp.float32),
            pltpu.VMEM((2 * width, width), jnp.float32),
            pltpu.SemaphoreType.DMA((SLOTS,)),
            pltpu.SemaphoreType.DMA((SLOTS,)),
            pltpu.SemaphoreType.DMA((SLOTS,)),
            pltpu.SemaphoreType.DMA((SLOTS,)),
            pltpu.SemaphoreType.DMA,
            pltpu.SemaphoreType.DMA,
            pltpu.SemaphoreType.DMA((n,)),
            pltpu.SemaphoreType.DMA((n,)),
            pltpu.SemaphoreType.DMA((n,)),
            pltpu.SemaphoreType.DMA((n,)),
        ],
        compiler_params=pltpu.CompilerParams(
            collective_id=0, has_side_effects=True, vmem_limit_bytes=48 * 1024 * 1024),
        cost_estimate=pl.CostEstimate(
            flops=SLOTS * 2 * count * count * (width + 48), bytes_accessed=4 * count * width,
            transcendentals=SLOTS * count * count),
        name="panels",
    )(directions, geom)
    return product, gram if reduce_here else lax.psum(gram, "blk")


def solution(mesh):
    in_specs = (P("blk", "rhs"), P("blk"), P("blk"), P("blk"))
    out_specs = (P("blk", "rhs"), P(None, "rhs"))
    body = functools.partial(shards, mesh.shape["blk"])
    return jax.shard_map(body, mesh=mesh, in_specs=in_specs, out_specs=out_specs, check_vma=False)
```

```python
import functools

import jax
import jax.numpy as jnp
from jax import lax
from jax.experimental import pallas as pl
from jax.experimental.pallas import tpu as pltpu
from jax.sharding import PartitionSpec as P

MESH = pl.DeviceIdType.MESH
COL_STEP = 512
ROW_STEP = 256
COL_GROUP = 1024
MIDDLE = 4.0
SOFTEN = 0.01
PIECES = 16
SLOTS = 7


def split_three(value):
    high = value.astype(jnp.bfloat16).astype(jnp.float32)
    rest = value - high
    mid = rest.astype(jnp.bfloat16).astype(jnp.float32)
    return high, mid, rest - mid


def panel_kernel(
    n, reduce_here, dirs_ref, geom_ref, product_ref, gram_ref,
    dirs, other, pieces, rows, turned_product, flat, partial, landed, summed,
    send_dirs, recv_dirs, send_geom, recv_geom, send_other, recv_other,
    send_part, recv_part, send_sum, recv_sum,
):
    me = lax.axis_index("blk")
    half = lax.axis_index("rhs")
    count = dirs_ref.shape[0]
    width = dirs_ref.shape[1]
    sign = 1 - 2 * lax.rem(me, 2)

    def block(offset):
        return lax.rem(me + offset * sign + n, n)

    pair = block(1)

    barrier = pltpu.get_barrier_semaphore()
    pl.semaphore_signal(barrier, inc=1, device_id=(me, 1 - half), device_id_type=MESH)
    if reduce_here:
        def greet(step, carry):
            pl.semaphore_signal(barrier, inc=1, device_id=(lax.rem(me + step, n), half), device_id_type=MESH)
            return carry

        lax.fori_loop(1, n, greet, 0)
    else:
        for offset in (1, -1, 2, -2, 3, -3):
            pl.semaphore_signal(barrier, inc=1, device_id=(block(offset), half), device_id_type=MESH)

    targets = ((1, pair), (2, block(-1)), (3, block(2)), (6, block(-3)))

    def dirs_copy(source, slot, target):
        return pltpu.make_async_remote_copy(
            src_ref=source, dst_ref=dirs.at[slot], send_sem=send_dirs.at[slot], recv_sem=recv_dirs.at[slot],
            device_id=(target, half), device_id_type=MESH)

    def geom_copy(source, slot, target):
        return pltpu.make_async_remote_copy(
            src_ref=source, dst_ref=pieces.at[slot], send_sem=send_geom.at[slot], recv_sem=recv_geom.at[slot],
            device_id=(target, half), device_id_type=MESH)

    axial = geom_ref[0:1, :] - MIDDLE
    cosine = geom_ref[1:2, :]
    sine = geom_ref[2:3, :]
    weight = geom_ref[3:4, :]
    scale = 1.0 / (weight * weight)
    norm = axial * axial + cosine * cosine + sine * sine + 0.5 * SOFTEN
    col_parts = (scale, norm * scale, axial * scale, cosine * scale, sine * scale)
    row_scale = scale * float(count)
    row_parts = (norm * row_scale, row_scale, -2.0 * axial * row_scale, -2.0 * cosine * row_scale,
                 -2.0 * sine * row_scale)
    flat[...] = jnp.zeros_like(flat)
    for at, part in enumerate(col_parts):
        for level, piece in enumerate(split_three(part)):
            flat[3 * at + level:3 * at + level + 1, :] = piece
    pieces[0] = flat[0:PIECES, :].astype(jnp.bfloat16)
    pl.semaphore_wait(barrier, n if reduce_here else 7)
    for slot, target in targets:
        geom_copy(pieces.at[0], slot, target).start()
    for start in range(0, count, 128):
        strip = dirs_ref[start:start + 128, :].astype(jnp.float32)
        dirs[0, :, start:start + 128] = strip.T.astype(jnp.bfloat16)
    for slot, target in targets:
        dirs_copy(dirs.at[0], slot, target).start()
    across = pltpu.make_async_remote_copy(
        src_ref=dirs.at[0], dst_ref=other, send_sem=send_other, recv_sem=recv_other,
        device_id=(me, 1 - half), device_id_type=MESH)
    across.start()

    flat[...] = jnp.zeros_like(flat)
    for at, part in enumerate(row_parts):
        for level, piece in enumerate(split_three(part)):
            for spot in range(3):
                place = PIECES * level + 3 * at + spot
                flat[place:place + 1, :] = piece
    rows[...] = flat[0:3 * PIECES, :].astype(jnp.bfloat16)
    turned_product[...] = jnp.zeros_like(turned_product)

    def tile(slot):
        def step(at, carry):
            features, block_dirs, chunks = [], [], []
            for sub in range(COL_GROUP // COL_STEP):
                here = pl.ds(pl.multiple_of(at * COL_GROUP + sub * COL_STEP, COL_STEP), COL_STEP)
                part = pieces[slot, :, here].astype(jnp.float32)
                features.append(jnp.concatenate([part, part, part], axis=0).T.astype(jnp.bfloat16))
                block_dirs.append(dirs[slot, :, here])
                chunks += [(sub, start) for start in range(0, count, ROW_STEP)]

            def squares(chunk):
                sub, start = chunk
                return jnp.dot(features[sub], rows[:, start:start + ROW_STEP], preferred_element_type=jnp.float32)

            square = squares(chunks[0])
            for (sub, start), following in zip(chunks, chunks[1:] + [None]):
                ahead = squares(following) if following else None
                values = lax.rsqrt(square).astype(jnp.bfloat16)
                turned_product[:, start:start + ROW_STEP] += jnp.dot(
                    block_dirs[sub], values, preferred_element_type=jnp.float32)
                square = ahead
            return carry

        lax.fori_loop(0, count // COL_GROUP, step, 0)

    def turn(slot, carry):
        @pl.when(slot > 0)
        def _():
            dirs_copy(dirs.at[0], slot, pair).wait_recv()
            geom_copy(pieces.at[0], slot, pair).wait_recv()

        @pl.when((slot == 2) | (slot == 3))
        def _():
            dirs_copy(dirs.at[slot], slot + 2, pair).start()
            geom_copy(pieces.at[slot], slot + 2, pair).start()

        tile(slot)
        return carry

    lax.fori_loop(0, SLOTS, turn, 0)

    across.wait()
    for start in range(0, count, 128):
        product_ref[start:start + 128, :] = turned_product[:, start:start + 128].T
    total = product_ref[...]
    high = total.astype(jnp.bfloat16)
    low = (total - high.astype(jnp.float32)).astype(jnp.bfloat16)
    inverse = 1.0 / (count * n)
    for place, value in ((half, dirs[0]), (1 - half, other[...])):
        inner = jnp.dot(value, high, preferred_element_type=jnp.float32)
        inner = inner + jnp.dot(value, low, preferred_element_type=jnp.float32)
        partial[pl.ds(pl.multiple_of(place * width, width), width), :] = inner * inverse

    if reduce_here:
        depth = landed.shape[1]

        def rows_of(owner):
            return pl.ds(pl.multiple_of(owner * depth, depth), depth)

        def part_copy(step):
            target = lax.rem(me + step, n)
            return pltpu.make_async_remote_copy(
                src_ref=partial.at[rows_of(target)], dst_ref=landed.at[step],
                send_sem=send_part.at[step], recv_sem=recv_part.at[step],
                device_id=(target, half), device_id_type=MESH)

        def sum_copy(step):
            target = lax.rem(me + step, n)
            return pltpu.make_async_remote_copy(
                src_ref=summed.at[rows_of(me)], dst_ref=summed.at[rows_of(me)],
                send_sem=send_sum.at[step], recv_sem=recv_sum.at[step],
                device_id=(target, half), device_id_type=MESH)

        def each(act):
            def run(step, carry):
                act(step)
                return carry

            lax.fori_loop(1, n, run, 0)

        each(lambda step: part_copy(step).start())
        landed[0] = partial[rows_of(me), :]
        each(lambda step: part_copy(step).wait_recv())
        summed[rows_of(me), :] = jnp.sum(landed[...], axis=0)
        each(lambda step: sum_copy(step).start())
        each(lambda step: sum_copy(step).wait_recv())
        gram_ref[...] = summed[...]
        each(lambda step: part_copy(step).wait_send())
        each(lambda step: sum_copy(step).wait_send())
    else:
        gram_ref[...] = partial[...]

    for slot in range(1, SLOTS):
        dirs_copy(dirs.at[0], slot, pair).wait_send()
        geom_copy(pieces.at[0], slot, pair).wait_send()


def shards(n, directions, axial_pos, azimuth, panel_area):
    count, width = directions.shape
    angle = azimuth.astype(jnp.float32)
    geom = jnp.stack([axial_pos.astype(jnp.float32), jnp.cos(angle), jnp.sin(angle), panel_area.astype(jnp.float32)])
    vmem = pl.BlockSpec(memory_space=pltpu.VMEM)
    reduce_here = (2 * width) % (8 * n) == 0
    depth = 2 * width // n if reduce_here else 8
    product, gram = pl.pallas_call(
        functools.partial(panel_kernel, n, reduce_here),
        out_shape=(
            jax.ShapeDtypeStruct((count, width), jnp.float32),
            jax.ShapeDtypeStruct((2 * width, width), jnp.float32),
        ),
        in_specs=[vmem, vmem],
        out_specs=(vmem, vmem),
        scratch_shapes=[
            pltpu.VMEM((SLOTS, width, count), jnp.bfloat16),
            pltpu.VMEM((width, count), jnp.bfloat16),
            pltpu.VMEM((SLOTS, PIECES, count), jnp.bfloat16),
            pltpu.VMEM((3 * PIECES, count), jnp.bfloat16),
            pltpu.VMEM((width, count), jnp.float32),
            pltpu.VMEM((128, count), jnp.float32),
            pltpu.VMEM((2 * width, width), jnp.float32),
            pltpu.VMEM((n, depth, width), jnp.float32),
            pltpu.VMEM((2 * width, width), jnp.float32),
            pltpu.SemaphoreType.DMA((SLOTS,)),
            pltpu.SemaphoreType.DMA((SLOTS,)),
            pltpu.SemaphoreType.DMA((SLOTS,)),
            pltpu.SemaphoreType.DMA((SLOTS,)),
            pltpu.SemaphoreType.DMA,
            pltpu.SemaphoreType.DMA,
            pltpu.SemaphoreType.DMA((n,)),
            pltpu.SemaphoreType.DMA((n,)),
            pltpu.SemaphoreType.DMA((n,)),
            pltpu.SemaphoreType.DMA((n,)),
        ],
        compiler_params=pltpu.CompilerParams(
            collective_id=0, has_side_effects=True, vmem_limit_bytes=48 * 1024 * 1024),
        cost_estimate=pl.CostEstimate(
            flops=SLOTS * 2 * count * count * (width + 48), bytes_accessed=4 * count * width,
            transcendentals=SLOTS * count * count),
        name="panels",
    )(directions, geom)
    return product, gram if reduce_here else lax.psum(gram, "blk")


def solution(mesh):
    in_specs = (P("blk", "rhs"), P("blk"), P("blk"), P("blk"))
    out_specs = (P("blk", "rhs"), P(None, "rhs"))
    body = functools.partial(shards, mesh.shape["blk"])
    return jax.shard_map(body, mesh=mesh, in_specs=in_specs, out_specs=out_specs, check_vma=False)
```
